256 devices in a mesh: dp: 4 (over y), coop: 64 (over x, z, core).
Axes of the slice: x: 4, y: 4, z: 8, core: 2. Of those that a mesh axis runs over, the one named last changes fastest.
Arguments:
- features: bfloat16 [131072, 512], P(('dp', 'coop')), parts along dimension 0, may hold values from -6 to 6
- self_first: bfloat16 [512, 256], replicated, may hold values from -0.25 to 0.25
- neighbour_first: bfloat16 [512, 256], replicated, may hold values from -0.25 to 0.25
- bias_first: float32 [256], replicated, may hold values from -3 to 3
- self_second: bfloat16 [256, 256], replicated, may hold values from -0.375 to 0.375
- neighbour_second: bfloat16 [256, 256], replicated, may hold values from -0.375 to 0.375
- bias_second: float32 [256], replicated, may hold values from -3 to 3
- request_first: int32 [256, 64, 16], P(('dp', 'coop')), parts along dimension 0, may hold values from 0 to 511, as said below
- adjacent_first: int32 [131072, 10], P(('dp', 'coop')), parts along dimension 0, may hold values from -1 to 1023, as said below
- request_second: int32 [256, 64, 16], P(('dp', 'coop')), parts along dimension 0, may hold values from 0 to 511, as said below
- adjacent_second: int32 [131072, 10], P(('dp', 'coop')), parts along dimension 0, may hold values from -1 to 1023, as said below
- request_edges: int32 [256, 64, 16], P(('dp', 'coop')), parts along dimension 0, may hold values from 0 to 511, as said below
- edge_source: int32 [131072], P(('dp', 'coop')), parts along dimension 0, may hold values from 0 to 511
- edge_target: int32 [131072], P(('dp', 'coop')), parts along dimension 0, may hold values from 0 to 1023, as said below
Outputs:
- embedding: bfloat16 [131072, 256], P(('dp', 'coop')), parts along dimension 0
- self_first_gradient: float32 [2048, 256], P('dp'), parts along dimension 0
- neighbour_first_gradient: float32 [2048, 256], P('dp'), parts along dimension 0
- bias_first_gradient: float32 [1024], P('dp'), parts along dimension 0
- self_second_gradient: float32 [1024, 256], P('dp'), parts along dimension 0
- neighbour_second_gradient: float32 [1024, 256], P('dp'), parts along dimension 0
- bias_second_gradient: float32 [1024], P('dp'), parts along dimension 0
The draws below stay inside these ranges and needn't reach their ends.
There are 4 independent parts, one for each index of `dp`. The reference program is written for one: setup_inputs(seed, part) draws one part's arguments, and reference() takes and returns one part's arrays. A program takes and returns all parts, laid end to end along the dimension named above; an argument that names none is the same for every part. Nothing has to cross between parts.
Inputs may be any that keep to these rules, and one draw needn't show every extreme that they name: For each device d and owner o the 16 entries request_first[d, o] are distinct rows of o. For each device d and owner o the 16 entries request_second[d, o] are distinct rows of o. For each device d and owner o the 16 entries request_edges[d, o] are distinct rows of o. `adjacent_first`: each row names 1 to 10 slots of its own device, valid entries first and -1 after; some rows have all 10. Slots named by no row of a device are never needed. In every draw some owner has all 16 of its slots named on every device, and every device names its first and its last slot. `adjacent_second`: as adjacent_first, for layer two. `edge_target`: slots of the edge requests of the edge's own device. In every draw some owner has all 16 of its slots named on every device, and every device names its first and its last slot.
All inputs are finite; a program needn't handle non-finite values.
Results may differ from the reference program's by a relative error of at most 0.006.
The reference program's roundings to bfloat16 on the way (of `proj_first`, `hidden`, `proj_second`, `outer_round`, `slot_second`, `inner_round` and `slot_first`) count: a program that leaves them out, or rounds other values in their place, can miss the bound.
Values may be sent and summed in bfloat16 or wider, within the bound.
A program may use at most 64 MiB of HBM per device.

```python
import jax
import jax.numpy as jnp
from jax import lax

F = 512
H = 256
K = 10
V_DEV = 512
E_DEV = 512
CAP = 16
CAP3 = 16
NODES = 32768
EDGES = 32768
N_COOP = 64


def plan_tables(key, salt, width):
    base = jax.random.fold_in(key, salt)
    key_hot, key_live, key_perm = jax.random.split(base, 3)
    hottest = jax.random.randint(key_hot, (), 0, N_COOP)
    live = jax.random.randint(key_live, (N_COOP, N_COOP), width // 2, width + 1)
    owners = jnp.arange(N_COOP)
    live = jnp.where(owners[None, :] == hottest, width, live)
    keys = jax.random.split(key_perm, N_COOP * N_COOP)
    rows = jax.vmap(lambda single: jax.random.permutation(single, V_DEV)[:width])(keys)
    return (rows.reshape(N_COOP, N_COOP, width).astype(jnp.int32), live, hottest)


def slot_draw(key, live, hottest, width, targets, fanout):
    key_owner, key_place, key_count = jax.random.split(key, 3)
    owner = jax.random.randint(key_owner, (N_COOP, targets, fanout), 0, N_COOP)
    devices = jnp.arange(N_COOP)[:, None, None]
    limit = live[devices, owner]
    place = jax.random.randint(key_place, (N_COOP, targets, fanout), 0, limit)
    slot = owner * width + place
    leading = hottest * width + jnp.arange(width)
    slot = slot.at[:, :width, 0].set(jnp.broadcast_to(leading[None, :], (N_COOP, width)))
    slot = slot.at[:, width, 0].set(N_COOP * width - 1)
    slot = slot.at[:, width + 1, 0].set(0)
    count = jax.random.randint(key_count, (N_COOP, targets), 1, fanout + 1)
    count = count.at[:, 0].set(fanout)
    valid = jnp.arange(fanout)[None, None, :] < count[:, :, None]
    return jnp.where(valid, slot, -1).astype(jnp.int32)


def draw_request_first(key, part):
    return plan_tables(key, 11, CAP)[0]


def draw_adjacent_first(key, part):
    rows, live, hottest = plan_tables(key, 11, CAP)
    key = jax.random.fold_in(key, 1)
    return slot_draw(key, live, hottest, CAP, V_DEV, K).reshape(N_COOP * V_DEV, K)


def draw_request_second(key, part):
    return plan_tables(key, 22, CAP)[0]


def draw_adjacent_second(key, part):
    rows, live, hottest = plan_tables(key, 22, CAP)
    key = jax.random.fold_in(key, 2)
    return slot_draw(key, live, hottest, CAP, V_DEV, K).reshape(N_COOP * V_DEV, K)


def draw_request_edges(key, part):
    return plan_tables(key, 33, CAP3)[0]


def draw_edge_target(key, part):
    rows, live, hottest = plan_tables(key, 33, CAP3)
    key = jax.random.fold_in(key, 3)
    return slot_draw(key, live, hottest, CAP3, E_DEV, 1).reshape(N_COOP * E_DEV)


def plant(result, own_key, least, top_value):
    dims = result.shape
    spot = [jax.random.randint(jax.random.fold_in(own_key, axis), (), 0, dims[axis]) for axis in range(len(dims))]
    result = result.at[tuple(spot)].set(least)
    longest = dims.index(max(dims))
    spot[longest] = (spot[longest] + 1) % dims[longest]
    return result.at[tuple(spot)].set(top_value)


def block_levels(rng, dims, cuts, least, largest):
    loudness = 1.0
    for position, shards_of in cuts:
        heights = jax.random.uniform(jax.random.fold_in(jax.random.fold_in(rng, 6), position), (shards_of,), jnp.float32, least / len(cuts), largest / len(cuts))
        loudness = loudness * jnp.repeat(jnp.exp(heights), dims[position] // shards_of).reshape((-1,) + (1,) * (len(dims) - 1 - position))
    return loudness


def centred(own_key, dims, deviation, most, cuts=(), kind=jnp.bfloat16):
    result = deviation * jax.random.normal(own_key, dims, jnp.float32)
    if cuts:
        result = result * block_levels(own_key, dims, cuts, -0.22, 0.18)
    return jnp.clip(result, -most, most).astype(kind)


def setup_inputs(seed: int = 0, part: int = 0) -> dict:
    streams_of = jax.random.split(jax.random.key(seed), 15)
    part_splits = jax.random.split(jax.random.fold_in(streams_of[14], part), 15)
    features = centred(part_splits[0], (NODES, F), 1.0, 6.0, ((0, 64),))
    self_first = centred(streams_of[1], (F, H), F ** -0.5, 0.25)
    neighbour_first = centred(streams_of[2], (F, H), F ** -0.5, 0.25)
    bias_first = centred(streams_of[3], (H,), 0.5, 3.0, (), jnp.float32)
    self_second = centred(streams_of[4], (H, H), H ** -0.5, 0.375)
    neighbour_second = centred(streams_of[5], (H, H), H ** -0.5, 0.375)
    bias_second = centred(streams_of[6], (H,), 0.5, 3.0, (), jnp.float32)
    request_first = draw_request_first(jax.random.fold_in(jax.random.fold_in(streams_of[14], part), 71), part)
    adjacent_first = draw_adjacent_first(jax.random.fold_in(jax.random.fold_in(streams_of[14], part), 71), part)
    request_second = draw_request_second(jax.random.fold_in(jax.random.fold_in(streams_of[14], part), 71), part)
    adjacent_second = draw_adjacent_second(jax.random.fold_in(jax.random.fold_in(streams_of[14], part), 71), part)
    request_edges = draw_request_edges(jax.random.fold_in(jax.random.fold_in(streams_of[14], part), 71), part)
    edge_source = plant(jax.random.randint(part_splits[12], (EDGES,), 0, V_DEV), jax.random.fold_in(part_splits[12], 1), 0, V_DEV - 1).astype(jnp.int32)
    edge_target = draw_edge_target(jax.random.fold_in(jax.random.fold_in(streams_of[14], part), 71), part)
    return {"features": features, "self_first": self_first, "neighbour_first": neighbour_first, "bias_first": bias_first, "self_second": self_second, "neighbour_second": neighbour_second, "bias_second": bias_second, "request_first": request_first, "adjacent_first": adjacent_first, "request_second": request_second, "adjacent_second": adjacent_second, "request_edges": request_edges, "edge_source": edge_source, "edge_target": edge_target}


def slot_vertices(request):
    owners = jnp.arange(N_COOP, dtype=jnp.int32)[None, :, None] * V_DEV
    return (owners + request).reshape(N_COOP, -1).astype(jnp.int32)


def neighbour_ids(request, adjacent):
    vertices = slot_vertices(request)
    table = adjacent.reshape(N_COOP, V_DEV, K)
    valid = table >= 0
    safe = jnp.where(valid, table, 0).astype(jnp.int32)
    found = jax.vmap(lambda rows, picks: rows[picks])(vertices, safe)
    return found.reshape(NODES, K), valid.reshape(NODES, K)


def neighbour_mean(rows, found, valid):
    count = jnp.sum(valid.astype(jnp.float32), axis=1)
    total = jnp.zeros((rows.shape[0], rows.shape[1]), jnp.float32)
    for column in range(K):
        picked = rows[found[:, column]].astype(jnp.float32)
        total = total + jnp.where(valid[:, column:column + 1], picked, 0.0)
    return total / count[:, None]


def slot_sums(grad, adjacent, width):
    slots = N_COOP * width
    table = adjacent.reshape(N_COOP, V_DEV, K)
    grads = grad.reshape(N_COOP, V_DEV, -1)

    def one_device(pair):
        local_grad, local_table = pair
        valid = local_table >= 0
        count = jnp.sum(valid.astype(jnp.float32), axis=1)
        scaled = local_grad / count[:, None]
        target = jnp.where(valid, local_table, slots).astype(jnp.int32)
        totals = jnp.zeros((slots + 1, local_grad.shape[1]), jnp.float32)
        for column in range(K):
            totals = totals.at[target[:, column]].add(scaled)
        return totals[:slots]

    return lax.map(one_device, (grads, table))


def vertex_totals(slot_rows, request):
    vertices = slot_vertices(request).reshape(-1)
    flat = slot_rows.astype(jnp.float32).reshape(vertices.shape[0], -1)
    return jnp.zeros((NODES, flat.shape[1]), jnp.float32).at[vertices].add(flat)


def reference(features, self_first, neighbour_first, bias_first, self_second, neighbour_second, bias_second, request_first, adjacent_first, request_second, adjacent_second, request_edges, edge_source, edge_target):
    highest = lax.Precision.HIGHEST
    found_first, valid_first = neighbour_ids(request_first, adjacent_first)
    found_second, valid_second = neighbour_ids(request_second, adjacent_second)
    proj_first = jnp.dot(features, neighbour_first, preferred_element_type=jnp.float32).astype(jnp.bfloat16)
    before = jnp.dot(features, self_first, preferred_element_type=jnp.float32) + neighbour_mean(proj_first, found_first, valid_first) + bias_first
    hidden = jnp.maximum(before, 0.0).astype(jnp.bfloat16)
    proj_second = jnp.dot(hidden, neighbour_second, preferred_element_type=jnp.float32).astype(jnp.bfloat16)
    embedding = (jnp.dot(hidden, self_second, preferred_element_type=jnp.float32) + neighbour_mean(proj_second, found_second, valid_second) + bias_second).astype(jnp.bfloat16)

    positions = jnp.arange(EDGES, dtype=jnp.int32)
    device = positions // E_DEV
    source = device * V_DEV + edge_source
    target = slot_vertices(request_edges)[device, edge_target]
    left = embedding[source].astype(jnp.float32)
    right = embedding[target].astype(jnp.float32)
    score = jnp.sum(left * right, axis=1) * (H ** -0.5)
    label = ((positions % E_DEV) < E_DEV // 2).astype(jnp.float32)
    coef = (jax.nn.sigmoid(score) - label) * ((EDGES * H) ** -0.5)
    outer_grad = jnp.zeros((NODES, H), jnp.float32)
    outer_grad = outer_grad.at[source].add(coef[:, None] * right)
    outer_grad = outer_grad.at[target].add(coef[:, None] * left)
    outer_round = outer_grad.astype(jnp.bfloat16)
    self_second_gradient = jnp.dot(hidden.T, outer_round, preferred_element_type=jnp.float32)
    bias_second_gradient = jnp.sum(outer_grad, axis=0)
    slot_second = slot_sums(outer_grad, adjacent_second, CAP).astype(jnp.bfloat16)
    second_totals = vertex_totals(slot_second, request_second)
    neighbour_second_gradient = jnp.dot(hidden.astype(jnp.float32).T, second_totals, precision=highest)
    back_hidden = jnp.dot(outer_round, self_second.T, preferred_element_type=jnp.float32)
    back_hidden = back_hidden + jnp.dot(second_totals, neighbour_second.astype(jnp.float32).T, precision=highest)
    inner = jnp.where(before > 0.0, back_hidden, 0.0)
    inner_round = inner.astype(jnp.bfloat16)
    self_first_gradient = jnp.dot(features.T, inner_round, preferred_element_type=jnp.float32)
    bias_first_gradient = jnp.sum(inner, axis=0)
    slot_first = slot_sums(inner, adjacent_first, CAP).astype(jnp.bfloat16)
    first_totals = vertex_totals(slot_first, request_first)
    neighbour_first_gradient = jnp.dot(features.astype(jnp.float32).T, first_totals, precision=highest)
    return (embedding, self_first_gradient, neighbour_first_gradient, bias_first_gradient, self_second_gradient, neighbour_second_gradient, bias_second_gradient)
```

```python
import functools

import jax
import jax.numpy as jnp
from jax import lax
from jax.experimental import pallas as pl
from jax.experimental.pallas import tpu as pltpu
from jax.sharding import PartitionSpec as P

MESH = pl.DeviceIdType.MESH
BF = jnp.bfloat16
F32 = jnp.float32
CHUNK = 256


def nn(a, b):
    return lax.dot_general(a, b, (((1,), (0,)), ((), ())), preferred_element_type=F32)


def nt(a, b):
    return lax.dot_general(a, b, (((1,), (1,)), ((), ())), preferred_element_type=F32)


def split(value):
    high = value.astype(BF)
    low = (value - high.astype(F32)).astype(BF)
    return high, low


def blocks(total, step, body):
    def one(i, carry):
        body(pl.ds(pl.multiple_of(i * step, step), step), i * step)
        return carry

    lax.fori_loop(0, total // step, one, 0)


def one_if(flag):
    return jnp.where(flag, 1.0, 0.0).astype(BF)


def kernel(
    peers,
    features,
    self_first,
    neighbour_first,
    bias_first,
    self_second,
    neighbour_second,
    bias_second,
    request_first,
    adjacent_first,
    request_second,
    adjacent_second,
    request_edges,
    edge_source,
    edge_target,
    embedding,
    out_self_first,
    out_neighbour_first,
    out_bias_first,
    out_self_second,
    out_neighbour_second,
    out_bias_second,
    ask_send,
    ask_recv,
    asked,
    a1,
    a1t,
    a2,
    a2t,
    p1,
    p1t,
    p2,
    p2t,
    p3,
    p3t,
    source_t,
    source,
    target_t,
    target,
    features_t,
    hidden_t,
    inv1,
    inv2,
    base,
    before,
    hidden,
    left,
    grad,
    own,
    totals,
    sends,
    recvs,
    bias_send,
    bias_recv,
    gradients,
    pair_recv,
    shard_send,
    shard_recv,
    final,
    send_sems,
    recv_sems,
):
    me = lax.axis_index("coop")
    chip = me // 2
    core = me % 2
    chips = peers // 2
    nodes, width = hidden.shape
    feats = features.shape[1]
    slots = a1.shape[1]
    edges = edge_source.shape[1]
    cap = slots // peers

    barrier = pltpu.get_barrier_semaphore()

    def greet(k, carry):
        pl.semaphore_signal(
            barrier, inc=1, device_id={"coop": (me + k) % peers}, device_id_type=MESH
        )
        return carry

    lax.fori_loop(1, peers, greet, 0)

    for d in range(peers):
        for n, request in enumerate((request_first, request_second, request_edges)):
            ask_send[d, :, cap * n : cap * (n + 1)] = request[d : d + 1, :]

    def counts(adjacent, matrix, inverse):
        step = 32

        def fill(rows, start):
            table = adjacent[rows, :]
            inverse[rows, :] = 1.0 / jnp.sum((table >= 0).astype(F32), axis=1, keepdims=True)
            lanes = lax.broadcasted_iota(jnp.int32, (step, slots), 1)
            total = jnp.zeros((step, slots), F32)
            for j in range(table.shape[1]):
                total = total + jnp.where(table[:, j : j + 1] == lanes, 1.0, 0.0)
            matrix[rows, :] = total.astype(BF)

        blocks(nodes, step, fill)

    def transpose(src, dst):
        def one(rows, start):
            dst[rows, :] = src[:, rows].T

        blocks(src.shape[1], 128, one)

    counts(adjacent_first, a1, inv1)
    counts(adjacent_second, a2, inv2)

    def node_base(rows, start):
        totals[rows, :] = nn(features[rows, :], neighbour_first[...])
        base[rows, :] = nn(features[rows, :], self_first[...]) + bias_first[...]

    blocks(nodes, CHUNK, node_base)
    projected = totals[...].astype(BF)
    hidden[...] = projected

    pl.semaphore_wait(barrier, peers - 1)

    def ask(k, carry):
        peer = (me + k) % peers
        pltpu.make_async_remote_copy(
            ask_send.at[peer],
            ask_recv.at[me],
            send_sems.at[0],
            recv_sems.at[0],
            device_id={"coop": peer},
            device_id_type=MESH,
        ).start()
        return carry

    lax.fori_loop(1, peers, ask, 0)
    ask_recv[pl.ds(me, 1)] = ask_send[pl.ds(me, 1)]
    others = pl.ds(0, peers - 1)
    pltpu.make_async_copy(ask_recv.at[others], ask_recv.at[others], recv_sems.at[0]).wait()
    for d in range(peers):
        asked[d : d + 1, :] = ask_recv[d]

    def picks(n, rows_matrix, columns_matrix):
        table = asked[...]
        high = table - (table % 16)
        parts = jnp.concatenate([high, table % 16], axis=1).astype(F32).astype(BF)
        step = min(CHUNK, slots)

        def one(rows, start):
            row = lax.broadcasted_iota(jnp.int32, (step, peers), 0) + start
            owner = lax.broadcasted_iota(jnp.int32, (step, peers), 1)
            spread = nn(one_if(row // cap == owner), parts)
            row = lax.broadcasted_iota(jnp.int32, spread.shape, 0) + start
            lane = lax.broadcasted_iota(jnp.int32, spread.shape, 1) % 128
            mine = jnp.where(lane == n * cap + row % cap, spread, 0.0).astype(BF)
            ones = jnp.ones((nodes, spread.shape[1]), BF)
            wanted = nt(mine, ones)
            rows_matrix[rows, :] = one_if(
                wanted == lax.broadcasted_iota(jnp.int32, wanted.shape, 1).astype(F32)
            )
            wanted_t = nt(ones, mine)
            columns_matrix[:, rows] = one_if(
                wanted_t == lax.broadcasted_iota(jnp.int32, wanted_t.shape, 0).astype(F32)
            )

        blocks(slots, step, one)

    def exchange(phase):
        def send(k, carry):
            peer = (me + k) % peers
            pltpu.make_async_remote_copy(
                sends.at[phase, pl.ds(pl.multiple_of(peer * cap, cap), cap)],
                recvs.at[phase, pl.ds(pl.multiple_of(me * cap, cap), cap)],
                send_sems.at[1 + phase],
                recv_sems.at[1 + phase],
                device_id={"coop": peer},
                device_id_type=MESH,
            ).start()
            return carry

        lax.fori_loop(1, peers, send, 0)
        mine = pl.ds(pl.multiple_of(me * cap, cap), cap)
        recvs[phase, mine, :] = sends[phase, mine, :]

    def arrived(phase):
        most = recvs.at[phase, pl.ds(0, (peers - 1) * cap)]
        pltpu.make_async_copy(most, most, recv_sems.at[1 + phase]).wait()

    def fill_rows(phase, matrix, rows_of):
        def one(rows, start):
            sends[phase, rows, :] = nn(matrix[rows, :], rows_of[...]).astype(BF)

        blocks(slots, min(CHUNK, slots), one)

    def fill_split(phase, matrix, value):
        high, low = split(value)

        def one(rows, start):
            part = matrix[rows, :]
            sends[phase, rows, :] = (nn(part, high) + nn(part, low)).astype(BF)

        blocks(slots, min(CHUNK, slots), one)

    picks(0, p1, p1t)
    fill_rows(0, p1, hidden)
    exchange(0)
    picks(1, p2, p2t)
    picks(2, p3, p3t)
    transpose(a1, a1t)
    transpose(a2, a2t)
    transpose(features, features_t)
    vertex = lax.broadcasted_iota(jnp.int32, (nodes, edges), 0)
    source_t[...] = one_if(vertex == edge_source[...])
    slot = lax.broadcasted_iota(jnp.int32, (slots, edges), 0)
    target_t[...] = one_if(slot == edge_target[...])
    transpose(source_t, source)
    transpose(target_t, target)
    arrived(0)

    def layer_one(rows, start):
        value = base[rows, :] + nn(a1[rows, :], recvs[0]) * inv1[rows, :]
        before[rows, :] = value
        hidden[rows, :] = jnp.maximum(value, 0.0).astype(BF)

    blocks(nodes, CHUNK, layer_one)

    def project(rows, start):
        left[rows, :] = nn(hidden[rows, :], neighbour_second[...]).astype(BF)

    blocks(nodes, CHUNK, project)
    fill_rows(1, p2, left)
    exchange(1)

    def second_base(rows, start):
        base[rows, :] = nn(hidden[rows, :], self_second[...]) + bias_second[...]

    blocks(nodes, CHUNK, second_base)
    transpose(hidden, hidden_t)
    arrived(1)

    def layer_two(rows, start):
        embedding[rows, :] = (
            base[rows, :] + nn(a2[rows, :], recvs[1]) * inv2[rows, :]
        ).astype(BF)

    blocks(nodes, CHUNK, layer_two)

    fill_rows(2, p3, embedding)
    exchange(2)

    def lefts(rows, start):
        left[rows, :] = nn(source[rows, :], embedding[...]).astype(BF)

    blocks(edges, CHUNK, lefts)
    arrived(2)

    def scores(rows, start):
        right = nn(target[rows, :], recvs[2])
        here = left[rows, :].astype(F32)
        score = jnp.sum(here * right, axis=1, keepdims=True) * width ** (-0.5)
        edge = lax.broadcasted_iota(jnp.int32, score.shape, 0) + start
        label = jnp.where(edge < edges // 2, 1.0, 0.0)
        coef = (jax.nn.sigmoid(score) - label) * (edges * peers * width) ** (-0.5)
        grad[rows, :] = coef * here
        own[rows, :] = coef * right

    blocks(edges, CHUNK, scores)
    fill_split(3, target_t, grad[...])
    exchange(3)
    high, low = split(own[...])
    totals[...] = nn(source_t[...], high) + nn(source_t[...], low)
    arrived(3)

    def outer(rows, start):
        grad[rows, :] = totals[rows, :] + nn(p3t[rows, :], recvs[3])

    blocks(nodes, CHUNK, outer)
    outer_round = grad[...].astype(BF)
    fill_split(4, a2t, grad[...] * inv2[...])
    exchange(4)
    bias_send[:, :, :width] = jnp.sum(grad[...], axis=0, keepdims=True)[None]
    self_rows = 2 * feats
    near_rows = 2 * feats + width
    gradients[self_rows : self_rows + width, :] = nn(hidden_t[...], outer_round)
    own[...] = nt(outer_round, self_second[...])
    arrived(4)

    def second_totals(rows, start):
        totals[rows, :] = nn(p2t[rows, :], recvs[4])

    blocks(nodes, CHUNK, second_totals)
    high, low = split(totals[...])
    value = own[...] + nt(high, neighbour_second[...]) + nt(low, neighbour_second[...])
    inner = jnp.where(before[...] > 0.0, value, 0.0)
    grad[...] = inner
    fill_split(5, a1t, inner * inv1[...])
    exchange(5)
    gradients[near_rows : near_rows + width, :] = nn(hidden_t[...], high) + nn(hidden_t[...], low)
    bias_send[:, :, width:] = jnp.sum(grad[...], axis=0, keepdims=True)[None]

    def bias(k, carry):
        peer = (me + k) % peers
        pltpu.make_async_remote_copy(
            bias_send.at[0],
            bias_recv.at[me],
            send_sems.at[7],
            recv_sems.at[7],
            device_id={"coop": peer},
            device_id_type=MESH,
        ).start()
        return carry

    lax.fori_loop(1, peers, bias, 0)
    bias_recv[pl.ds(me, 1)] = bias_send[...]
    inner_round = grad[...].astype(BF)

    def self_gradient(rows, start):
        gradients[rows, :] = nn(features_t[rows, :], inner_round)

    blocks(feats, CHUNK, self_gradient)
    pltpu.make_async_copy(bias_recv.at[others], bias_recv.at[others], recv_sems.at[7]).wait()
    total = bias_recv[0]
    for d in range(1, peers):
        total = total + bias_recv[d]
    out_bias_second[...] = total[:, :width]
    out_bias_first[...] = total[:, width:]
    arrived(5)

    def first_totals(rows, start):
        totals[rows, :] = nn(p1t[rows, :], recvs[5])

    blocks(nodes, CHUNK, first_totals)
    high, low = split(totals[...])

    def near_gradient(rows, start):
        part = features_t[rows, :]
        gradients[pl.ds(pl.multiple_of(start + feats, CHUNK), CHUNK), :] = nn(part, high) + nn(
            part, low
        )

    blocks(feats, CHUNK, near_gradient)

    half = gradients.shape[0] // 2
    share = half // chips
    kept = pl.ds(pl.multiple_of(core * half, 8), half)
    given = pl.ds(pl.multiple_of((1 - core) * half, 8), half)
    partner = chip * 2 + 1 - core
    pair = pltpu.make_async_remote_copy(
        gradients.at[given],
        pair_recv,
        send_sems.at[8],
        recv_sems.at[8],
        device_id={"coop": partner},
        device_id_type=MESH,
    )
    pair.start()
    pair.wait_recv()
    shard_send[...] = gradients[kept, :] + pair_recv[...]

    def scatter(k, carry):
        to = (chip + k) % chips
        pltpu.make_async_remote_copy(
            shard_send.at[pl.ds(pl.multiple_of(to * share, 8), share)],
            shard_recv.at[pl.ds(pl.multiple_of(chip * share, 8), share)],
            send_sems.at[9],
            recv_sems.at[9],
            device_id={"coop": to * 2 + core},
            device_id_type=MESH,
        ).start()
        return carry

    lax.fori_loop(1, chips, scatter, 0)
    here = pl.ds(pl.multiple_of(chip * share, 8), share)
    shard_recv[here, :] = shard_send[here, :]
    most = shard_recv.at[pl.ds(0, (chips - 1) * share)]
    pltpu.make_async_copy(most, most, recv_sems.at[9]).wait()
    total = shard_recv[0:share, :]
    for c in range(1, chips):
        total = total + shard_recv[c * share : (c + 1) * share, :]
    place = pl.ds(pl.multiple_of(core * half + chip * share, 8), share)
    final[place, :] = total

    def gather(k, carry):
        to = (chip + k) % chips
        pltpu.make_async_remote_copy(
            final.at[place],
            final.at[place],
            send_sems.at[10],
            recv_sems.at[10],
            device_id={"coop": to * 2 + core},
            device_id_type=MESH,
        ).start()
        return carry

    lax.fori_loop(1, chips, gather, 0)
    pltpu.make_async_copy(most, most, recv_sems.at[10]).wait()
    back = pltpu.make_async_remote_copy(
        final.at[kept],
        final.at[kept],
        send_sems.at[11],
        recv_sems.at[11],
        device_id={"coop": partner},
        device_id_type=MESH,
    )
    back.start()
    back.wait_recv()
    out_self_first[...] = final[:feats, :]
    out_neighbour_first[...] = final[feats : 2 * feats, :]
    out_self_second[...] = final[self_rows : self_rows + width, :]
    out_neighbour_second[...] = final[near_rows : near_rows + width, :]

    pltpu.make_async_copy(ask_send.at[others], ask_send.at[others], send_sems.at[0]).wait()
    for phase in range(6):
        sent = sends.at[phase, pl.ds(0, (peers - 1) * cap)]
        pltpu.make_async_copy(sent, sent, send_sems.at[1 + phase]).wait()
    pltpu.make_async_copy(bias_recv.at[others], bias_recv.at[others], send_sems.at[7]).wait()
    pair.wait_send()
    pltpu.make_async_copy(most, most, send_sems.at[9]).wait()
    pltpu.make_async_copy(most, most, send_sems.at[10]).wait()
    back.wait_send()


def per_device(
    features,
    self_first,
    neighbour_first,
    bias_first,
    self_second,
    neighbour_second,
    bias_second,
    request_first,
    adjacent_first,
    request_second,
    adjacent_second,
    request_edges,
    edge_source,
    edge_target,
):
    nodes, feats = features.shape
    width = self_first.shape[1]
    _, peers, cap = request_first.shape
    slots = peers * cap
    edges = edge_source.shape[0]
    rows = 2 * feats + 2 * width
    vmem = pltpu.VMEM
    scratch = [
        vmem((peers, 1, 128), jnp.int32),
        vmem((peers, 1, 128), jnp.int32),
        vmem((peers, 128), jnp.int32),
        vmem((nodes, slots), BF),
        vmem((slots, nodes), BF),
        vmem((nodes, slots), BF),
        vmem((slots, nodes), BF),
        vmem((slots, nodes), BF),
        vmem((nodes, slots), BF),
        vmem((slots, nodes), BF),
        vmem((nodes, slots), BF),
        vmem((slots, nodes), BF),
        vmem((nodes, slots), BF),
        vmem((nodes, edges), BF),
        vmem((edges, nodes), BF),
        vmem((slots, edges), BF),
        vmem((edges, slots), BF),
        vmem((feats, nodes), BF),
        vmem((width, nodes), BF),
        vmem((nodes, 1), F32),
        vmem((nodes, 1), F32),
        vmem((nodes, width), F32),
        vmem((nodes, width), F32),
        vmem((nodes, width), BF),
        vmem((nodes, width), BF),
        vmem((nodes, width), F32),
        vmem((nodes, width), F32),
        vmem((nodes, width), F32),
        vmem((6, slots, width), BF),
        vmem((6, slots, width), BF),
        vmem((1, 1, 2 * width), F32),
        vmem((peers, 1, 2 * width), F32),
        vmem((rows, width), F32),
        vmem((rows // 2, width), F32),
        vmem((rows // 2, width), F32),
        vmem((rows // 2, width), F32),
        vmem((rows, width), F32),
        pltpu.SemaphoreType.DMA((12,)),
        pltpu.SemaphoreType.DMA((12,)),
    ]
    results = pl.pallas_call(
        functools.partial(kernel, peers),
        out_shape=(
            jax.ShapeDtypeStruct((nodes, width), BF),
            jax.ShapeDtypeStruct((feats, width), F32),
            jax.ShapeDtypeStruct((feats, width), F32),
            jax.ShapeDtypeStruct((1, width), F32),
            jax.ShapeDtypeStruct((width, width), F32),
            jax.ShapeDtypeStruct((width, width), F32),
            jax.ShapeDtypeStruct((1, width), F32),
        ),
        in_specs=[pl.BlockSpec(memory_space=vmem)] * 14,
        out_specs=[pl.BlockSpec(memory_space=vmem)] * 7,
        scratch_shapes=scratch,
        compiler_params=pltpu.CompilerParams(
            collective_id=0, has_side_effects=True, vmem_limit_bytes=52 * 2**20
        ),
    )(
        features,
        self_first,
        neighbour_first,
        bias_first.reshape(1, width),
        self_second,
        neighbour_second,
        bias_second.reshape(1, width),
        request_first[0],
        adjacent_first,
        request_second[0],
        adjacent_second,
        request_edges[0],
        edge_source.reshape(1, edges),
        edge_target.reshape(1, edges),
    )
    return (
        results[0],
        results[1],
        results[2],
        results[3].reshape(width),
        results[4],
        results[5],
        results[6].reshape(width),
    )


def solution(mesh):
    in_specs = (
        P(("dp", "coop"), None),
        P(),
        P(),
        P(),
        P(),
        P(),
        P(),
        P(("dp", "coop"), None, None),
        P(("dp", "coop"), None),
        P(("dp", "coop"), None, None),
        P(("dp", "coop"), None),
        P(("dp", "coop"), None, None),
        P(("dp", "coop")),
        P(("dp", "coop")),
    )
    out_specs = (
        P(("dp", "coop"), None),
        P("dp", None),
        P("dp", None),
        P("dp"),
        P("dp", None),
        P("dp", None),
        P("dp"),
    )
    return jax.shard_map(
        per_device, mesh=mesh, in_specs=in_specs, out_specs=out_specs, check_vma=False
    )
```

```python
import functools

import jax
import jax.numpy as jnp
from jax import lax
from jax.experimental import pallas as pl
from jax.experimental.pallas import tpu as pltpu
from jax.sharding import PartitionSpec as P

MESH = pl.DeviceIdType.MESH
BF = jnp.bfloat16
F32 = jnp.float32
CHUNK = 256
TRAVEL = jnp.bfloat16
LOAD_ORDER = (7, 9, 11, 0, 2, 8, 10, 12, 13, 1, 3, 4, 5, 6)


def nn(a, b):
    return lax.dot_general(a, b, (((1,), (0,)), ((), ())), preferred_element_type=F32)


def nt(a, b):
    return lax.dot_general(a, b, (((1,), (1,)), ((), ())), preferred_element_type=F32)


def split(value):
    high = value.astype(BF)
    low = (value - high.astype(F32)).astype(BF)
    return high, low


def blocks(total, step, body):
    def one(i, carry):
        body(pl.ds(pl.multiple_of(i * step, step), step), i * step)
        return carry

    lax.fori_loop(0, total // step, one, 0)


def one_if(flag):
    return jnp.where(flag, 1.0, 0.0).astype(BF)


def kernel(
    peers,
    *refs,
):
    arguments, refs = refs[:14], refs[14:]
    held, refs = refs[3:17], refs[:3] + refs[17:]
    step_through(peers, arguments, held, *refs)


def step_through(
    peers,
    arguments,
    held,
    out_embedding,
    out_gradients,
    out_bias,
    embedding,
    bias_total,
    out_sems,
    held_sems,
    ask_send,
    ask_recv,
    asked,
    a1,
    a1t,
    a2,
    a2t,
    p1,
    p2,
    p2t,
    p3,
    p3t,
    source_t,
    source,
    target_t,
    target,
    features_t,
    arrived_t,
    hidden_t,
    inv1,
    inv2,
    base,
    before,
    hidden,
    left,
    grad,
    own,
    totals,
    slot_first,
    sends,
    recvs,
    highs,
    lows,
    feature_send,
    feature_recv,
    bias_send,
    bias_near,
    bias_held,
    bias_recv,
    gradients,
    pair_send,
    pair_recv,
    shard_send,
    shard_recv,
    final,
    send_sems,
    recv_sems,
):
    me = lax.axis_index("coop")
    loads = [
        pltpu.make_async_copy(argument, place, held_sems.at[n])
        for n, (argument, place) in enumerate(zip(arguments, held))
    ]
    for n in LOAD_ORDER:
        loads[n].start()
    (
        features,
        self_first,
        neighbour_first,
        bias_first,
        self_second,
        neighbour_second,
        bias_second,
        request_first,
        adjacent_first,
        request_second,
        adjacent_second,
        request_edges,
        edge_source,
        edge_target,
    ) = held
    chip = me // 2
    core = me % 2
    chips = peers // 2
    nodes, width = hidden.shape
    feats = features.shape[1]
    slots = a1.shape[1]
    edges = edge_source.shape[1]
    cap = slots // peers
    step = min(CHUNK, slots)

    barrier = pltpu.get_barrier_semaphore()

    def greet(k, carry):
        pl.semaphore_signal(
            barrier, inc=1, device_id={"coop": (me + k) % peers}, device_id_type=MESH
        )
        return carry

    lax.fori_loop(1, peers, greet, 0)

    def count(adjacent, matrix_t):
        tall = 32
        table = adjacent[...]

        def fill(rows, start):
            slot = lax.broadcasted_iota(jnp.int32, (tall, nodes), 0) + start
            total = jnp.zeros((tall, nodes), F32)
            for j in range(table.shape[0]):
                total = total + jnp.where(table[j : j + 1, :] == slot, 1.0, 0.0)
            matrix_t[rows, :] = total.astype(BF)

        blocks(slots, tall, fill)

    def transpose(src, dst):
        def one(rows, start):
            shape = (128, src.shape[1])
            row = lax.broadcasted_iota(jnp.int32, shape, 0) + start
            dst[rows, :] = nt(
                one_if(row == lax.broadcasted_iota(jnp.int32, shape, 1)), src[...]
            ).astype(BF)

        blocks(src.shape[1], 128, one)

    def inverse(matrix, result):
        def one(rows, start):
            result[rows, :] = 1.0 / nn(matrix[rows, :], jnp.ones((slots, width), BF))

        blocks(nodes, CHUNK, one)

    for n in LOAD_ORDER[:7]:
        loads[n].wait()
    for n, request in enumerate((request_first, request_second, request_edges)):
        wanted = request[...].T
        for d in range(peers):
            ask_send[d, :, cap * n : cap * (n + 1)] = wanted[d : d + 1, :]

    def project_first(rows, start):
        left[rows, :] = nn(features[rows, :], neighbour_first[...]).astype(BF)

    blocks(nodes, CHUNK, project_first)
    count(adjacent_first, a1t)
    count(adjacent_second, a2t)
    for n in LOAD_ORDER[7:]:
        loads[n].wait()
    vertex = lax.broadcasted_iota(jnp.int32, (nodes, edges), 0)
    source_t[...] = one_if(vertex == edge_source[...])
    slot = lax.broadcasted_iota(jnp.int32, (slots, edges), 0)
    target_t[...] = one_if(slot == edge_target[...])

    pl.semaphore_wait(barrier, peers - 1)

    def ask(k, carry):
        peer = (me + k) % peers
        pltpu.make_async_remote_copy(
            ask_send.at[peer],
            ask_recv.at[me],
            send_sems.at[10],
            recv_sems.at[10],
            device_id={"coop": peer},
            device_id_type=MESH,
        ).start()
        return carry

    lax.fori_loop(1, peers, ask, 0)
    ask_recv[pl.ds(me, 1)] = ask_send[pl.ds(me, 1)]

    def base_first(rows, start):
        base[rows, :] = nn(features[rows, :], self_first[...]) + bias_first[...]

    blocks(nodes, CHUNK, base_first)
    transpose(a1t, a1)
    inverse(a1, inv1)

    others = pl.ds(0, peers - 1)
    pltpu.make_async_copy(ask_recv.at[others], ask_recv.at[others], recv_sems.at[10]).wait()
    for d in range(peers):
        asked[d : d + 1, :] = ask_recv[d]

    def mine(n, start):
        table = asked[...]
        low = table % 16
        parts = jnp.concatenate([table - low, low], axis=1).astype(F32).astype(BF)
        row = lax.broadcasted_iota(jnp.int32, (step, peers), 0) + start
        owner = lax.broadcasted_iota(jnp.int32, (step, peers), 1)
        spread = nn(one_if(row // cap == owner), parts)
        row = lax.broadcasted_iota(jnp.int32, spread.shape, 0) + start
        lane = lax.broadcasted_iota(jnp.int32, spread.shape, 1) % 128
        return jnp.where(lane == n * cap + row % cap, spread, 0.0).astype(BF)

    def picks(n, matrix):
        def one(rows, start):
            part = mine(n, start)
            wanted = nt(part, jnp.ones((nodes, part.shape[1]), BF))
            matrix[rows, :] = one_if(
                wanted == lax.broadcasted_iota(jnp.int32, wanted.shape, 1).astype(F32)
            )

        blocks(slots, step, one)

    def picks_t(n, matrix):
        def one(rows, start):
            part = mine(n, start)
            wanted = nt(jnp.ones((nodes, part.shape[1]), BF), part)
            matrix[:, rows] = one_if(
                wanted == lax.broadcasted_iota(jnp.int32, wanted.shape, 0).astype(F32)
            )

        blocks(slots, step, one)

    def exchange(phase, side):
        def send(k, carry):
            peer = (me + k) % peers
            pltpu.make_async_remote_copy(
                sends.at[phase, side, pl.ds(pl.multiple_of(peer * cap, cap), cap)],
                recvs.at[phase, side, pl.ds(pl.multiple_of(me * cap, cap), cap)],
                send_sems.at[2 * phase + side],
                recv_sems.at[2 * phase + side],
                device_id={"coop": peer},
                device_id_type=MESH,
            ).start()
            return carry

        lax.fori_loop(1, peers, send, 0)
        mine = pl.ds(pl.multiple_of(me * cap, cap), cap)
        recvs[phase, side, mine, :] = sends[phase, side, mine, :]

    def sent(phase, side):
        most = sends.at[phase, side, pl.ds(0, (peers - 1) * cap)]
        pltpu.make_async_copy(most, most, send_sems.at[2 * phase + side]).wait()

    def arrived(phase, side):
        most = recvs.at[phase, side, pl.ds(0, (peers - 1) * cap)]
        pltpu.make_async_copy(most, most, recv_sems.at[2 * phase + side]).wait()

    def send_features(part):
        def send(k, carry):
            peer = (me + 4 * k + part) % peers
            pltpu.make_async_remote_copy(
                feature_send.at[pl.ds(pl.multiple_of(peer * cap, cap), cap)],
                feature_recv.at[pl.ds(pl.multiple_of(me * cap, cap), cap)],
                send_sems.at[11],
                recv_sems.at[11],
                device_id={"coop": peer},
                device_id_type=MESH,
            ).start()
            return carry

        lax.fori_loop(1 if part == 0 else 0, peers // 4, send, 0)

    half = width // 2
    sides = (slice(0, half), slice(half, width))

    def fill(phase, matrix, rows_of):
        def one(rows, start):
            part = nn(matrix[rows, :], rows_of[...]).astype(BF)
            for side in range(2):
                sends[phase, side, rows, :] = part[:, sides[side]]

        blocks(slots, step, one)
        for side in range(2):
            exchange(phase, side)

    def fill_side(phase, side, matrix, *pieces):
        def one(rows, start):
            part = matrix[rows, :]
            total = nn(part, pieces[0])
            for piece in pieces[1:]:
                total = total + nn(part, piece)
            sends[phase, side, rows, :] = total.astype(BF)

        blocks(slots, step, one)
        exchange(phase, side)

    picks(0, p1)
    fill(0, p1, left)

    def gather_features(rows, start):
        feature_send[rows, :] = nn(p1[rows, :], features[...]).astype(BF)

    blocks(slots, step, gather_features)
    here = pl.ds(pl.multiple_of(me * cap, cap), cap)
    feature_recv[here, :] = feature_send[here, :]
    picks(1, p2)
    sent(0, 0)
    sent(0, 1)
    send_features(0)
    for side in range(2):
        arrived(0, side)
        cols = sides[side]

        def layer_one(rows, start):
            value = base[rows, cols] + nn(a1[rows, :], recvs[0, side]) * inv1[rows, cols]
            before[rows, cols] = value
            part = jnp.maximum(value, 0.0).astype(BF)
            hidden[rows, cols] = part
            more = nn(part, neighbour_second[cols, :])
            if side == 0:
                totals[rows, :] = more
            else:
                left[rows, :] = (totals[rows, :] + more).astype(BF)

        blocks(nodes, CHUNK, layer_one)

    fill(1, p2, left)

    def second_base(rows, start):
        base[rows, :] = nn(hidden[rows, :], self_second[...]) + bias_second[...]

    blocks(nodes, CHUNK, second_base)
    transpose(a2t, a2)
    inverse(a2, inv2)
    picks(2, p3)
    for side in range(2):
        arrived(1, side)
        cols = sides[side]

        def layer_two(rows, start):
            embedding[rows, cols] = (
                base[rows, cols] + nn(a2[rows, :], recvs[1, side]) * inv2[rows, cols]
            ).astype(BF)

        blocks(nodes, CHUNK, layer_two)
        fill_side(2, side, p3, embedding[:, cols])
    leave = [
        pltpu.make_async_copy(embedding, out_embedding, out_sems.at[0]),
        pltpu.make_async_copy(bias_total, out_bias, out_sems.at[1]),
        pltpu.make_async_copy(final, out_gradients, out_sems.at[2]),
    ]
    leave[0].start()
    transpose(source_t, source)
    transpose(target_t, target)

    def lefts(rows, start):
        left[rows, :] = nn(source[rows, :], embedding[...]).astype(BF)

    blocks(edges, CHUNK, lefts)
    transpose(hidden, hidden_t)
    picks_t(2, p3t)
    for side in range(2):
        sent(1, side)
        sent(2, side)
    send_features(1)
    arrived(2, 0)

    def first_scores(rows, start):
        right = nn(target[rows, :], recvs[2, 0])
        own[rows, sides[0]] = right
        grad[rows, sides[0]] = left[rows, sides[0]].astype(F32) * right

    blocks(edges, CHUNK, first_scores)
    arrived(2, 1)

    def scores(rows, start):
        right = nn(target[rows, :], recvs[2, 1])
        here = left[rows, :].astype(F32)
        products = grad[rows, sides[0]] + here[:, sides[1]] * right
        score = jnp.sum(products, axis=1, keepdims=True) * width ** (-0.5)
        edge = lax.broadcasted_iota(jnp.int32, score.shape, 0) + start
        label = jnp.where(edge < edges // 2, 1.0, 0.0)
        coef = (jax.nn.sigmoid(score) - label) * (edges * peers * width) ** (-0.5)
        grad[rows, :] = coef * here
        own[rows, sides[0]] = coef * own[rows, sides[0]]
        own[rows, sides[1]] = coef * right

    blocks(edges, CHUNK, scores)
    for side in range(2):
        fill_side(3, side, target_t, *split(grad[:, sides[side]]))
    high, low = split(own[...])
    totals[...] = nn(source_t[...], high) + nn(source_t[...], low)
    picks_t(1, p2t)
    transpose(features, features_t)
    sent(3, 0)
    sent(3, 1)
    send_features(2)
    for side in range(2):
        arrived(3, side)
        cols = sides[side]

        def outer(rows, start):
            grad[rows, cols] = totals[rows, cols] + nn(p3t[rows, :], recvs[3, side])

        blocks(nodes, CHUNK, outer)
        fill_side(4, side, a2t, *split(grad[:, cols] * inv2[:, cols]))
    send_features(3)
    bias_send[:, :, :width] = jnp.sum(grad[...], axis=0, keepdims=True)[None]
    outer_round = grad[...].astype(BF)
    second = slice(half, half + width)
    gradients[1, :width, second] = nn(hidden_t[...], outer_round)
    own[...] = nt(outer_round, self_second[...])
    for side in range(2):
        arrived(4, side)
        cols = sides[side]

        def second_totals(rows, start):
            value = nn(p2t[rows, :], recvs[4, side])
            high, low = split(value)
            highs[rows, cols] = high
            lows[rows, cols] = low
            weight = neighbour_second[:, cols]
            value = own[rows, :] + nt(high, weight) + nt(low, weight)
            if side == 0:
                own[rows, :] = value
            else:
                grad[rows, :] = jnp.where(before[rows, :] > 0.0, value, 0.0)

        blocks(nodes, CHUNK, second_totals)

    most = feature_recv.at[pl.ds(0, (peers - 1) * cap)]
    pltpu.make_async_copy(most, most, recv_sems.at[11]).wait()
    transpose(feature_recv, arrived_t)
    inner_round = grad[...].astype(BF)
    high, low = split(grad[...] * inv1[...])

    def slot_totals(rows, start):
        part = a1t[rows, :]
        slot_first[rows, :] = (nn(part, high) + nn(part, low)).astype(BF)

    blocks(slots, step, slot_totals)

    def first_gradients(rows, start):
        gradients[0, rows, :width] = nn(features_t[rows, :], inner_round)
        near = nn(arrived_t[rows, :], slot_first[...])
        gradients[0, rows, width:] = near[:, :half]
        gradients[1, rows, :half] = near[:, half:]

    blocks(feats, CHUNK, first_gradients)
    gradients[1, width:, second] = nn(hidden_t[...], highs[...]) + nn(hidden_t[...], lows[...])
    bias_send[:, :, width:] = jnp.sum(grad[...], axis=0, keepdims=True)[None]

    share = feats // chips
    partner = chip * 2 + 1 - core
    pair_send[...] = gradients[1 - core].astype(pair_send.dtype)
    pair = pltpu.make_async_remote_copy(
        pair_send,
        pair_recv,
        send_sems.at[13],
        recv_sems.at[13],
        device_id={"coop": partner},
        device_id_type=MESH,
    )
    pair.start()
    bias_pair = pltpu.make_async_remote_copy(
        bias_send,
        bias_near,
        send_sems.at[12],
        recv_sems.at[12],
        device_id={"coop": partner},
        device_id_type=MESH,
    )
    bias_pair.start()
    pair.wait_recv()
    shard_send[...] = (gradients[core] + pair_recv[...].astype(F32)).astype(shard_send.dtype)

    def scatter(k, carry):
        to = (chip + k) % chips
        pltpu.make_async_remote_copy(
            shard_send.at[pl.ds(pl.multiple_of(to * share, share), share)],
            shard_recv.at[pl.ds(pl.multiple_of(chip * share, share), share)],
            send_sems.at[14],
            recv_sems.at[14],
            device_id={"coop": to * 2 + core},
            device_id_type=MESH,
        ).start()
        return carry

    lax.fori_loop(1, chips, scatter, 0)
    place = pl.ds(pl.multiple_of(chip * share, share), share)
    shard_recv[place, :] = shard_send[place, :]
    bias_pair.wait_recv()
    bias_held[...] = bias_send[...] + bias_near[...]

    def spread_bias(k, carry):
        to = (chip + k) % chips
        pltpu.make_async_remote_copy(
            bias_held.at[0],
            bias_recv.at[chip],
            send_sems.at[17],
            recv_sems.at[17],
            device_id={"coop": to * 2 + core},
            device_id_type=MESH,
        ).start()
        return carry

    lax.fori_loop(1, chips, spread_bias, 0)
    bias_recv[pl.ds(chip, 1)] = bias_held[...]
    most = shard_recv.at[pl.ds(0, (chips - 1) * share)]
    pltpu.make_async_copy(most, most, recv_sems.at[14]).wait()
    total = shard_recv[0:share, :].astype(F32)
    for c in range(1, chips):
        total = total + shard_recv[c * share : (c + 1) * share, :].astype(F32)
    final[core, place, :] = total.astype(final.dtype)

    def gather(k, carry):
        to = (chip + k) % chips
        pltpu.make_async_remote_copy(
            final.at[core, place],
            final.at[core, place],
            send_sems.at[15],
            recv_sems.at[15],
            device_id={"coop": to * 2 + core},
            device_id_type=MESH,
        ).start()
        return carry

    lax.fori_loop(1, chips, gather, 0)
    far = pl.ds(0, chips - 1)
    pltpu.make_async_copy(bias_recv.at[far], bias_recv.at[far], recv_sems.at[17]).wait()
    total = bias_recv[0]
    for c in range(1, chips):
        total = total + bias_recv[c]
    bias_total[...] = total
    leave[1].start()
    pltpu.make_async_copy(most, most, recv_sems.at[15]).wait()
    back = pltpu.make_async_remote_copy(
        final.at[core],
        final.at[core],
        send_sems.at[16],
        recv_sems.at[16],
        device_id={"coop": partner},
        device_id_type=MESH,
    )
    back.start()
    back.wait_recv()
    leave[2].start()

    sent(4, 0)
    sent(4, 1)
    pltpu.make_async_copy(ask_send.at[others], ask_send.at[others], send_sems.at[10]).wait()
    gone = feature_send.at[pl.ds(0, (peers - 1) * cap)]
    pltpu.make_async_copy(gone, gone, send_sems.at[11]).wait()
    bias_pair.wait_send()
    pltpu.make_async_copy(bias_recv.at[far], bias_recv.at[far], send_sems.at[17]).wait()
    pair.wait_send()
    pltpu.make_async_copy(most, most, send_sems.at[14]).wait()
    pltpu.make_async_copy(most, most, send_sems.at[15]).wait()
    back.wait_send()
    for copy in leave:
        copy.wait()


def finish(
    in_embedding,
    in_gradients,
    in_bias,
    out_embedding,
    out_self_first,
    out_neighbour_first,
    out_bias_first,
    out_self_second,
    out_neighbour_second,
    out_bias_second,
    embedding,
    bias,
    self_first,
    neighbour_first,
    self_second,
    neighbour_second,
    gradients,
    sems,
):
    loads = [
        pltpu.make_async_copy(in_gradients, gradients, sems.at[7]),
        pltpu.make_async_copy(in_embedding, embedding, sems.at[8]),
        pltpu.make_async_copy(in_bias, bias, sems.at[9]),
    ]
    for load in loads:
        load.start()
    width = embedding.shape[1]
    edge = width // 2
    copies = []

    def leave(src, dst):
        copies.append(pltpu.make_async_copy(src, dst, sems.at[len(copies)]))
        copies[-1].start()

    loads[0].wait()
    self_first[...] = gradients[0, :, :width].astype(F32)
    leave(self_first, out_self_first)
    neighbour_first[:, :edge] = gradients[0, :, width:].astype(F32)
    neighbour_first[:, edge:] = gradients[1, :, :edge].astype(F32)
    leave(neighbour_first, out_neighbour_first)
    loads[1].wait()
    leave(embedding, out_embedding)
    self_second[...] = gradients[1, :width, edge:].astype(F32)
    leave(self_second, out_self_second)
    neighbour_second[...] = gradients[1, width:, edge:].astype(F32)
    leave(neighbour_second, out_neighbour_second)
    loads[2].wait()
    leave(bias.at[:, :width], out_bias_second)
    leave(bias.at[:, width:], out_bias_first)
    for copy in copies:
        copy.wait()


def per_device(
    features,
    self_first,
    neighbour_first,
    bias_first,
    self_second,
    neighbour_second,
    bias_second,
    request_first,
    adjacent_first,
    request_second,
    adjacent_second,
    request_edges,
    edge_source,
    edge_target,
):
    nodes, feats = features.shape
    width = self_first.shape[1]
    _, peers, cap = request_first.shape
    slots = peers * cap
    edges = edge_source.shape[0]
    wide = 3 * width // 2
    arguments = (
        features,
        self_first,
        neighbour_first,
        bias_first.reshape(1, width),
        self_second,
        neighbour_second,
        bias_second.reshape(1, width),
        request_first[0].T,
        adjacent_first.T,
        request_second[0].T,
        adjacent_second.T,
        request_edges[0].T,
        edge_source.reshape(1, edges),
        edge_target.reshape(1, edges),
    )
    vmem = pltpu.VMEM
    scratch = [vmem(a.shape, a.dtype) for a in arguments] + [
        vmem((nodes, width), BF),
        vmem((1, 2 * width), F32),
        pltpu.SemaphoreType.DMA((3,)),
        pltpu.SemaphoreType.DMA((14,)),
        vmem((peers, 1, 128), jnp.int32),
        vmem((peers, 1, 128), jnp.int32),
        vmem((peers, 128), jnp.int32),
        vmem((nodes, slots), BF),
        vmem((slots, nodes), BF),
        vmem((nodes, slots), BF),
        vmem((slots, nodes), BF),
        vmem((slots, nodes), BF),
        vmem((slots, nodes), BF),
        vmem((nodes, slots), BF),
        vmem((slots, nodes), BF),
        vmem((nodes, slots), BF),
        vmem((nodes, edges), BF),
        vmem((edges, nodes), BF),
        vmem((slots, edges), BF),
        vmem((edges, slots), BF),
        vmem((feats, nodes), BF),
        vmem((feats, slots), BF),
        vmem((width, nodes), BF),
        vmem((nodes, width), F32),
        vmem((nodes, width), F32),
        vmem((nodes, width), F32),
        vmem((nodes, width), F32),
        vmem((nodes, width), BF),
        vmem((nodes, width), BF),
        vmem((nodes, width), F32),
        vmem((nodes, width), F32),
        vmem((nodes, width), F32),
        vmem((slots, width), BF),
        vmem((5, 2, slots, width // 2), BF),
        vmem((5, 2, slots, width // 2), BF),
        vmem((nodes, width), BF),
        vmem((nodes, width), BF),
        vmem((slots, feats), BF),
        vmem((slots, feats), BF),
        vmem((1, 1, 2 * width), F32),
        vmem((1, 1, 2 * width), F32),
        vmem((1, 1, 2 * width), F32),
        vmem((peers // 2, 1, 2 * width), F32),
        vmem((2, feats, wide), F32),
        vmem((feats, wide), TRAVEL),
        vmem((feats, wide), TRAVEL),
        vmem((feats, wide), TRAVEL),
        vmem((feats, wide), TRAVEL),
        vmem((2, feats, wide), TRAVEL),
        pltpu.SemaphoreType.DMA((18,)),
        pltpu.SemaphoreType.DMA((18,)),
    ]
    summed = pl.pallas_call(
        functools.partial(kernel, peers),
        out_shape=(
            jax.ShapeDtypeStruct((nodes, width), BF),
            jax.ShapeDtypeStruct((2, feats, wide), TRAVEL),
            jax.ShapeDtypeStruct((1, 2 * width), F32),
        ),
        in_specs=[pl.BlockSpec(memory_space=pltpu.HBM)] * 14,
        out_specs=[pl.BlockSpec(memory_space=pltpu.HBM)] * 3,
        scratch_shapes=scratch,
        compiler_params=pltpu.CompilerParams(
            collective_id=0, has_side_effects=True, vmem_limit_bytes=60 * 2**20
        ),
    )(*arguments)
    results = pl.pallas_call(
        finish,
        out_shape=(
            jax.ShapeDtypeStruct((nodes, width), BF),
            jax.ShapeDtypeStruct((feats, width), F32),
            jax.ShapeDtypeStruct((feats, width), F32),
            jax.ShapeDtypeStruct((1, width), F32),
            jax.ShapeDtypeStruct((width, width), F32),
            jax.ShapeDtypeStruct((width, width), F32),
            jax.ShapeDtypeStruct((1, width), F32),
        ),
        in_specs=[pl.BlockSpec(memory_space=pltpu.HBM)] * 3,
        out_specs=[pl.BlockSpec(memory_space=pltpu.HBM)] * 7,
        scratch_shapes=[
            vmem((nodes, width), BF),
            vmem((1, 2 * width), F32),
            vmem((feats, width), F32),
            vmem((feats, width), F32),
            vmem((width, width), F32),
            vmem((width, width), F32),
            vmem((2, feats, wide), TRAVEL),
            pltpu.SemaphoreType.DMA((10,)),
        ],
        compiler_params=pltpu.CompilerParams(vmem_limit_bytes=60 * 2**20),
    )(*summed)
    return (
        results[0],
        results[1],
        results[2],
        results[3].reshape(width),
        results[4],
        results[5],
        results[6].reshape(width),
    )


def solution(mesh):
    in_specs = (
        P(("dp", "coop"), None),
        P(),
        P(),
        P(),
        P(),
        P(),
        P(),
        P(("dp", "coop"), None, None),
        P(("dp", "coop"), None),
        P(("dp", "coop"), None, None),
        P(("dp", "coop"), None),
        P(("dp", "coop"), None, None),
        P(("dp", "coop")),
        P(("dp", "coop")),
    )
    out_specs = (
        P(("dp", "coop"), None),
        P("dp", None),
        P("dp", None),
        P("dp"),
        P("dp", None),
        P("dp", None),
        P("dp"),
    )
    return jax.shard_map(
        per_device, mesh=mesh, in_specs=in_specs, out_specs=out_specs, check_vma=False
    )
```

```python
import functools

import jax
import jax.numpy as jnp
from jax import lax
from jax.experimental import pallas as pl
from jax.experimental.pallas import tpu as pltpu
from jax.sharding import PartitionSpec as P

MESH = pl.DeviceIdType.MESH
BF = jnp.bfloat16
F32 = jnp.float32
CHUNK = 256
XS = 4
ZS = 8
TRAVEL = jnp.bfloat16
LOAD_ORDER = (7, 9, 11, 0, 2, 8, 10, 12, 13, 1, 3, 4, 5, 6)


def far_x(i):
    return (1 - i // 2) * (2 + i) + (i // 2) * (3 - i)


def far_z(j):
    return ZS // 2 + (j // 2) * (1 - 2 * (j % 2)) - j % 2


def every(body):
    def one(n, carry):
        body(far_x(n // ZS), far_z(n % ZS))
        return carry

    lax.fori_loop(0, XS * ZS, one, 0)


def nn(a, b):
    return lax.dot_general(a, b, (((1,), (0,)), ((), ())), preferred_element_type=F32)


def nt(a, b):
    return lax.dot_general(a, b, (((1,), (1,)), ((), ())), preferred_element_type=F32)


def split(value):
    high = value.astype(BF)
    low = (value - high.astype(F32)).astype(BF)
    return high, low


def blocks(total, step, body):
    def one(i, carry):
        body(pl.ds(pl.multiple_of(i * step, step), step), i * step)
        return carry

    lax.fori_loop(0, total // step, one, 0)


def one_if(flag):
    return jnp.where(flag, 1.0, 0.0).astype(BF)


def kernel(
    peers,
    *refs,
):
    arguments, refs = refs[:14], refs[14:]
    held, refs = refs[4:18], refs[:4] + refs[18:]
    step_through(peers, arguments, held, *refs)


def step_through(
    peers,
    arguments,
    held,
    out_embedding,
    out_one,
    out_two,
    out_bias,
    embedding,
    bias_total,
    out_sems,
    held_sems,
    ask_send,
    ask_recv,
    asked,
    a1,
    a1t,
    a2,
    a2t,
    p1,
    p1t,
    p2,
    p2t,
    p3,
    p3t,
    source_t,
    source,
    target_t,
    target,
    features_t,
    hidden_t,
    inv1,
    inv2,
    base,
    before,
    hidden,
    left,
    grad,
    own,
    totals,
    sends,
    recvs,
    highs,
    lows,
    bias_send,
    bias_near,
    bias_held,
    bias_recv,
    grads_one,
    pair_one,
    shards_one,
    final_one,
    grads_two,
    pair_two,
    shards_two,
    final_two,
    send_sems,
    recv_sems,
):
    me = lax.axis_index("coop")
    chip = me // 2
    core = me % 2
    chips = peers // 2
    barrier = pltpu.get_barrier_semaphore()

    def chip_at(x, z):
        return (chip // ZS + x) % XS * ZS + (chip + z) % ZS

    def to_all(start):
        def both(x, z):
            to = chip_at(x, z) * 2
            start(to + 1 - core)

            @pl.when(to + core != me)
            def _():
                start(to + core)

        every(both)

    def to_others(start):
        def one(x, z):
            to = chip_at(x, z)

            @pl.when(to != chip)
            def _():
                start(to)

        every(one)

    def greet(peer):
        pl.semaphore_signal(barrier, inc=1, device_id={"coop": peer}, device_id_type=MESH)

    to_all(greet)
    loads = [
        pltpu.make_async_copy(argument, place, held_sems.at[n])
        for n, (argument, place) in enumerate(zip(arguments, held))
    ]
    for n in LOAD_ORDER:
        loads[n].start()
    (
        features,
        self_first,
        neighbour_first,
        bias_first,
        self_second,
        neighbour_second,
        bias_second,
        request_first,
        adjacent_first,
        request_second,
        adjacent_second,
        request_edges,
        edge_source,
        edge_target,
    ) = held
    nodes, width = hidden.shape
    feats = features.shape[1]
    slots = a1.shape[1]
    edges = edge_source.shape[1]
    cap = slots // peers
    step = slots // XS

    def count(adjacent, matrix_t):
        tall = 32
        table = adjacent[...]

        def fill(rows, start):
            slot = lax.broadcasted_iota(jnp.int32, (tall, nodes), 0) + start
            total = jnp.zeros((tall, nodes), F32)
            for j in range(table.shape[0]):
                total = total + jnp.where(table[j : j + 1, :] == slot, 1.0, 0.0)
            matrix_t[rows, :] = total.astype(BF)

        blocks(slots, tall, fill)

    def transpose(src, dst):
        def one(rows, start):
            shape = (128, src.shape[1])
            row = lax.broadcasted_iota(jnp.int32, shape, 0) + start
            dst[rows, :] = nt(
                one_if(row == lax.broadcasted_iota(jnp.int32, shape, 1)), src[...]
            ).astype(BF)

        blocks(src.shape[1], 128, one)

    def inverse(matrix, result):
        def one(rows, start):
            result[rows, :] = 1.0 / nn(matrix[rows, :], jnp.ones((slots, width), BF))

        blocks(nodes, CHUNK, one)

    for n in LOAD_ORDER[:5]:
        loads[n].wait()
    for n, request in enumerate((request_first, request_second, request_edges)):
        wanted = request[...].T
        for d in range(peers):
            ask_send[d, :, cap * n : cap * (n + 1)] = wanted[d : d + 1, :]

    def project_first(rows, start):
        left[rows, :] = nn(features[rows, :], neighbour_first[...]).astype(BF)

    blocks(nodes, CHUNK, project_first)
    for n in LOAD_ORDER[5:]:
        loads[n].wait()

    pl.semaphore_wait(barrier, peers - 1)

    def ask(peer):
        pltpu.make_async_remote_copy(
            ask_send.at[peer],
            ask_recv.at[me],
            send_sems.at[15],
            recv_sems.at[15],
            device_id={"coop": peer},
            device_id_type=MESH,
        ).start()

    to_all(ask)
    ask_recv[pl.ds(me, 1)] = ask_send[pl.ds(me, 1)]

    def base_first(rows, start):
        base[rows, :] = nn(features[rows, :], self_first[...]) + bias_first[...]

    blocks(nodes, CHUNK, base_first)
    count(adjacent_first, a1t)

    others = pl.ds(0, peers - 1)
    pltpu.make_async_copy(ask_recv.at[others], ask_recv.at[others], recv_sems.at[15]).wait()
    for d in range(peers):
        asked[d : d + 1, :] = ask_recv[d]

    def mine(n, start):
        table = asked[...]
        low = table % 16
        parts = jnp.concatenate([table - low, low], axis=1).astype(F32).astype(BF)
        row = lax.broadcasted_iota(jnp.int32, (step, peers), 0) + start
        owner = lax.broadcasted_iota(jnp.int32, (step, peers), 1)
        spread = nn(one_if(row // cap == owner), parts)
        row = lax.broadcasted_iota(jnp.int32, spread.shape, 0) + start
        lane = lax.broadcasted_iota(jnp.int32, spread.shape, 1) % 128
        return jnp.where(lane == n * cap + row % cap, spread, 0.0).astype(BF)

    def picks(n, matrix):
        def one(rows, start):
            part = mine(n, start)
            wanted = nt(part, jnp.ones((nodes, part.shape[1]), BF))
            matrix[rows, :] = one_if(
                wanted == lax.broadcasted_iota(jnp.int32, wanted.shape, 1).astype(F32)
            )

        blocks(slots, step, one)

    def picks_t(n, matrix):
        def one(rows, start):
            part = mine(n, start)
            wanted = nt(jnp.ones((nodes, part.shape[1]), BF), part)
            matrix[:, rows] = one_if(
                wanted == lax.broadcasted_iota(jnp.int32, wanted.shape, 0).astype(F32)
            )

        blocks(slots, step, one)

    def block(phase, side, peer):
        return pltpu.make_async_remote_copy(
            sends.at[phase, side, pl.ds(pl.multiple_of(peer * cap, cap), cap)],
            recvs.at[phase, side, pl.ds(pl.multiple_of(me * cap, cap), cap)],
            send_sems.at[2 * phase + side],
            recv_sems.at[2 * phase + side],
            device_id={"coop": peer},
            device_id_type=MESH,
        )

    group = 2 * ZS

    def ship(phase, side, body):
        def one(i, carry):
            x = (chip // ZS + far_x(i)) % XS
            start = x * step
            if body is not None:
                body(pl.ds(pl.multiple_of(start, step), step), start)

            def send(j, carry):
                to = x * group + (chip + far_z(j)) % ZS * 2
                block(phase, side, to + 1 - core).start()

                @pl.when(to + core != me)
                def _():
                    block(phase, side, to + core).start()

                return carry

            lax.fori_loop(0, ZS, send, 0)
            return carry

        lax.fori_loop(0, XS, one, 0)
        mine = pl.ds(pl.multiple_of(me * cap, cap), cap)
        recvs[phase, side, mine, :] = sends[phase, side, mine, :]

    def sent(phase, side):
        most = sends.at[phase, side, pl.ds(0, (peers - 1) * cap)]
        pltpu.make_async_copy(most, most, send_sems.at[2 * phase + side]).wait()

    def arrived(phase, side):
        most = recvs.at[phase, side, pl.ds(0, (peers - 1) * cap)]
        pltpu.make_async_copy(most, most, recv_sems.at[2 * phase + side]).wait()

    half = width // 2
    sides = (slice(0, half), slice(half, width))

    def fill(phase, matrix, rows_of):
        def one(rows, start):
            part = nn(matrix[rows, :], rows_of[...]).astype(BF)
            for side in range(2):
                sends[phase, side, rows, :] = part[:, sides[side]]

        ship(phase, 0, one)
        ship(phase, 1, None)

    def fill_side(phase, side, matrix, rows_of):
        def one(rows, start):
            sends[phase, side, rows, :] = nn(matrix[rows, :], rows_of).astype(BF)

        ship(phase, side, one)

    def joined(value):
        return jnp.concatenate(split(value), axis=1)

    def folded(value):
        return value[:, :half] + value[:, half:]

    def fill_split(phase, side, matrix, value):
        pieces = joined(value)

        def one(rows, start):
            sends[phase, side, rows, :] = folded(nn(matrix[rows, :], pieces)).astype(BF)

        ship(phase, side, one)

    picks(0, p1)
    fill(0, p1, left)

    transpose(a1t, a1)
    inverse(a1, inv1)
    picks(1, p2)
    count(adjacent_second, a2t)
    transpose(a2t, a2)
    inverse(a2, inv2)
    picks(2, p3)
    for side in range(2):
        arrived(0, side)
        cols = sides[side]

        def layer_one(rows, start):
            value = base[rows, cols] + nn(a1[rows, :], recvs[0, side]) * inv1[rows, cols]
            before[rows, cols] = value
            part = jnp.maximum(value, 0.0).astype(BF)
            hidden[rows, cols] = part
            more = nn(part, neighbour_second[cols, :])
            if side == 0:
                totals[rows, :] = more
            else:
                left[rows, :] = (totals[rows, :] + more).astype(BF)

        blocks(nodes, CHUNK, layer_one)

    fill(1, p2, left)

    def second_base(rows, start):
        base[rows, :] = nn(hidden[rows, :], self_second[...]) + bias_second[...]

    blocks(nodes, CHUNK, second_base)
    vertex = lax.broadcasted_iota(jnp.int32, (nodes, edges), 0)
    source_t[...] = one_if(vertex == edge_source[...])
    slot = lax.broadcasted_iota(jnp.int32, (slots, edges), 0)
    target_t[...] = one_if(slot == edge_target[...])
    transpose(source_t, source)
    transpose(target_t, target)
    transpose(hidden, hidden_t)
    for side in range(2):
        arrived(1, side)
        cols = sides[side]

        def layer_two(rows, start):
            embedding[rows, cols] = (
                base[rows, cols] + nn(a2[rows, :], recvs[1, side]) * inv2[rows, cols]
            ).astype(BF)

        blocks(nodes, CHUNK, layer_two)
        fill_side(2, side, p3, embedding[:, cols])
    leave = [
        pltpu.make_async_copy(embedding, out_embedding, out_sems.at[0]),
        pltpu.make_async_copy(bias_total, out_bias, out_sems.at[1]),
        pltpu.make_async_copy(final_one, out_one, out_sems.at[2]),
        pltpu.make_async_copy(final_two, out_two, out_sems.at[3]),
    ]
    leave[0].start()

    def lefts(rows, start):
        left[rows, :] = nn(source[rows, :], embedding[...]).astype(BF)

    blocks(edges, CHUNK, lefts)
    picks_t(2, p3t)
    transpose(features, features_t)
    picks_t(1, p2t)
    arrived(2, 0)

    def first_scores(rows, start):
        right = nn(target[rows, :], recvs[2, 0])
        own[rows, sides[0]] = right
        grad[rows, sides[0]] = left[rows, sides[0]].astype(F32) * right

    blocks(edges, CHUNK, first_scores)
    arrived(2, 1)

    def scores(rows, start):
        right = nn(target[rows, :], recvs[2, 1])
        here = left[rows, :].astype(F32)
        products = grad[rows, sides[0]] + here[:, sides[1]] * right
        score = jnp.sum(products, axis=1, keepdims=True) * width ** (-0.5)
        edge = lax.broadcasted_iota(jnp.int32, score.shape, 0) + start
        label = jnp.where(edge < edges // 2, 1.0, 0.0)
        coef = (jax.nn.sigmoid(score) - label) * (edges * peers * width) ** (-0.5)
        grad[rows, :] = coef * here
        own[rows, sides[0]] = coef * own[rows, sides[0]]
        own[rows, sides[1]] = coef * right

    blocks(edges, CHUNK, scores)
    for side in range(2):
        fill_split(3, side, target_t, grad[:, sides[side]])
    high, low = split(own[...])
    totals[...] = nn(source_t[...], high) + nn(source_t[...], low)
    picks_t(0, p1t)
    for side in range(2):
        arrived(3, side)
        cols = sides[side]

        def outer(rows, start):
            grad[rows, cols] = totals[rows, cols] + nn(p3t[rows, :], recvs[3, side])

        blocks(nodes, CHUNK, outer)
        fill_split(4, side, a2t, grad[:, cols] * inv2[:, cols])
    bias_send[:, :, :width] = jnp.sum(grad[...], axis=0, keepdims=True)[None]
    outer_round = grad[...].astype(BF)
    grads_one[1, :width, :] = nn(hidden_t[...], outer_round)
    own[...] = nt(outer_round, self_second[...])
    for side in range(2):
        arrived(4, side)
        cols = sides[side]
        weight = neighbour_second[:, cols]
        weights = jnp.concatenate([weight, weight], axis=1)

        def second_totals(rows, start):
            value = nn(p2t[rows, :], recvs[4, side])
            high, low = split(value)
            highs[rows, cols] = high
            lows[rows, cols] = low
            value = own[rows, :] + nt(jnp.concatenate([high, low], axis=1), weights)
            if side == 0:
                own[rows, :] = value
            else:
                grad[rows, :] = jnp.where(before[rows, :] > 0.0, value, 0.0)

        blocks(nodes, CHUNK, second_totals)

    for side in range(2):
        cols = sides[side]
        fill_split(5, side, a1t, grad[:, cols] * inv1[:, cols])
    inner_round = grad[...].astype(BF)

    def self_gradient(rows, start):
        grads_one[0, rows, :] = nn(features_t[rows, :], inner_round)

    blocks(feats, CHUNK, self_gradient)
    grads_one[1, width:, :] = nn(hidden_t[...], highs[...]) + nn(hidden_t[...], lows[...])

    share = feats // chips
    place = pl.ds(pl.multiple_of(chip * share, share), share)
    partner = chip * 2 + 1 - core

    class Summing:
        def __init__(self, grads, pair, shards, final, first_sem):
            self.grads, self.pair, self.shards, self.final = grads, pair, shards, final
            self.sem = first_sem
            self.swap = self.to_partner(pair.at[0], pair.at[1], 0)
            self.back = self.to_partner(final.at[core], final.at[core], 3)

        def to_partner(self, src, dst, n):
            return pltpu.make_async_remote_copy(
                src,
                dst,
                send_sems.at[self.sem + n],
                recv_sems.at[self.sem + n],
                device_id={"coop": partner},
                device_id_type=MESH,
            )

        def to_chips(self, src_of, dst, n):
            def send(to):
                pltpu.make_async_remote_copy(
                    src_of(to),
                    dst,
                    send_sems.at[self.sem + n],
                    recv_sems.at[self.sem + n],
                    device_id={"coop": to * 2 + core},
                    device_id_type=MESH,
                ).start()

            to_others(send)

        def all_of(self, sem):
            most = self.shards.at[1, pl.ds(0, (chips - 1) * share)]
            pltpu.make_async_copy(most, most, sem).wait()

        def start(self):
            self.pair[0] = self.grads[1 - core].astype(TRAVEL)
            self.swap.start()

        def add_pair(self):
            self.swap.wait_recv()
            self.shards[0] = (self.grads[core] + self.pair[1].astype(F32)).astype(TRAVEL)

        def scatter(self):
            self.to_chips(
                lambda to: self.shards.at[0, pl.ds(pl.multiple_of(to * share, share), share)],
                self.shards.at[1, place],
                1,
            )
            self.shards[1, place, :] = self.shards[0, place, :]

        def gather(self):
            self.all_of(recv_sems.at[self.sem + 1])
            total = self.shards[1, 0:share, :].astype(F32)
            for c in range(1, chips):
                total = total + self.shards[1, c * share : (c + 1) * share, :].astype(F32)
            self.final[core, place, :] = total.astype(TRAVEL)
            mine = self.final.at[core, place]
            self.to_chips(lambda to: mine, mine, 2)

        def give_back(self):
            self.all_of(recv_sems.at[self.sem + 2])
            self.back.start()

        def left(self):
            self.swap.wait_send()
            self.all_of(send_sems.at[self.sem + 1])
            self.all_of(send_sems.at[self.sem + 2])
            self.back.wait_send()

    one = Summing(grads_one, pair_one, shards_one, final_one, 16)
    two = Summing(grads_two, pair_two, shards_two, final_two, 20)
    one.start()
    bias_send[:, :, width:] = jnp.sum(grad[...], axis=0, keepdims=True)[None]
    bias_pair = pltpu.make_async_remote_copy(
        bias_send,
        bias_near,
        send_sems.at[13],
        recv_sems.at[13],
        device_id={"coop": partner},
        device_id_type=MESH,
    )
    bias_pair.start()
    one.add_pair()
    bias_pair.wait_recv()
    bias_held[...] = bias_send[...] + bias_near[...]
    sent(5, 0)
    sent(5, 1)
    one.scatter()

    def spread_bias(to):
        pltpu.make_async_remote_copy(
            bias_held.at[0],
            bias_recv.at[chip],
            send_sems.at[14],
            recv_sems.at[14],
            device_id={"coop": to * 2 + core},
            device_id_type=MESH,
        ).start()

    to_others(spread_bias)
    bias_recv[pl.ds(chip, 1)] = bias_held[...]
    for side in range(2):
        arrived(5, side)
        pieces = joined(nn(p1t[...], recvs[5, side]))

        def near_gradient(rows, start):
            grads_two[side, rows, :] = folded(nn(features_t[rows, :], pieces))

        blocks(feats, CHUNK, near_gradient)
    two.start()
    two.add_pair()
    two.scatter()
    one.gather()
    far = pl.ds(0, chips - 1)
    pltpu.make_async_copy(bias_recv.at[far], bias_recv.at[far], recv_sems.at[14]).wait()
    total = bias_recv[0]
    for c in range(1, chips):
        total = total + bias_recv[c]
    bias_total[...] = total
    leave[1].start()
    two.gather()
    one.give_back()
    two.give_back()
    one.back.wait_recv()
    leave[2].start()
    two.back.wait_recv()
    leave[3].start()

    pltpu.make_async_copy(ask_send.at[others], ask_send.at[others], send_sems.at[15]).wait()
    for phase in range(5):
        sent(phase, 0)
        sent(phase, 1)
    bias_pair.wait_send()
    pltpu.make_async_copy(bias_recv.at[far], bias_recv.at[far], send_sems.at[14]).wait()
    one.left()
    two.left()
    for copy in leave:
        copy.wait()


def finish(
    in_embedding,
    in_one,
    in_two,
    in_bias,
    out_embedding,
    out_self_first,
    out_neighbour_first,
    out_bias_first,
    out_self_second,
    out_neighbour_second,
    out_bias_second,
    embedding,
    one,
    two,
    bias,
    self_first,
    neighbour_first,
    self_second,
    neighbour_second,
    sems,
):
    loads = [
        pltpu.make_async_copy(src, dst, sems.at[7 + n])
        for n, (src, dst) in enumerate(
            ((in_one, one), (in_two, two), (in_embedding, embedding), (in_bias, bias))
        )
    ]
    for load in loads:
        load.start()
    width = embedding.shape[1]
    half = width // 2
    copies = []

    def leave(src, dst):
        copies.append(pltpu.make_async_copy(src, dst, sems.at[len(copies)]))
        copies[-1].start()

    loads[0].wait()
    self_first[...] = one[0].astype(F32)
    leave(self_first, out_self_first)
    loads[1].wait()
    neighbour_first[:, :half] = two[0].astype(F32)
    neighbour_first[:, half:] = two[1].astype(F32)
    leave(neighbour_first, out_neighbour_first)
    loads[2].wait()
    leave(embedding, out_embedding)
    self_second[...] = one[1, :width].astype(F32)
    leave(self_second, out_self_second)
    neighbour_second[...] = one[1, width:].astype(F32)
    leave(neighbour_second, out_neighbour_second)
    loads[3].wait()
    leave(bias.at[:, :width], out_bias_second)
    leave(bias.at[:, width:], out_bias_first)
    for copy in copies:
        copy.wait()


def per_device(
    features,
    self_first,
    neighbour_first,
    bias_first,
    self_second,
    neighbour_second,
    bias_second,
    request_first,
    adjacent_first,
    request_second,
    adjacent_second,
    request_edges,
    edge_source,
    edge_target,
):
    nodes, feats = features.shape
    width = self_first.shape[1]
    _, peers, cap = request_first.shape
    slots = peers * cap
    edges = edge_source.shape[0]
    arguments = (
        features,
        self_first,
        neighbour_first,
        bias_first.reshape(1, width),
        self_second,
        neighbour_second,
        bias_second.reshape(1, width),
        request_first[0].T,
        adjacent_first.T,
        request_second[0].T,
        adjacent_second.T,
        request_edges[0].T,
        edge_source.reshape(1, edges),
        edge_target.reshape(1, edges),
    )
    vmem = pltpu.VMEM
    scratch = [vmem(a.shape, a.dtype) for a in arguments] + [
        vmem((nodes, width), BF),
        vmem((1, 2 * width), F32),
        pltpu.SemaphoreType.DMA((4,)),
        pltpu.SemaphoreType.DMA((14,)),
        vmem((peers, 1, 128), jnp.int32),
        vmem((peers, 1, 128), jnp.int32),
        vmem((peers, 128), jnp.int32),
        vmem((nodes, slots), BF),
        vmem((slots, nodes), BF),
        vmem((nodes, slots), BF),
        vmem((slots, nodes), BF),
        vmem((slots, nodes), BF),
        vmem((nodes, slots), BF),
        vmem((slots, nodes), BF),
        vmem((nodes, slots), BF),
        vmem((slots, nodes), BF),
        vmem((nodes, slots), BF),
        vmem((nodes, edges), BF),
        vmem((edges, nodes), BF),
        vmem((slots, edges), BF),
        vmem((edges, slots), BF),
        vmem((feats, nodes), BF),
        vmem((width, nodes), BF),
        vmem((nodes, width), F32),
        vmem((nodes, width), F32),
        vmem((nodes, width), F32),
        vmem((nodes, width), F32),
        vmem((nodes, width), BF),
        vmem((nodes, width), BF),
        vmem((nodes, width), F32),
        vmem((nodes, width), F32),
        vmem((nodes, width), F32),
        vmem((6, 2, slots, width // 2), BF),
        vmem((6, 2, slots, width // 2), BF),
        vmem((nodes, width), BF),
        vmem((nodes, width), BF),
        vmem((1, 1, 2 * width), F32),
        vmem((1, 1, 2 * width), F32),
        vmem((1, 1, 2 * width), F32),
        vmem((peers // 2, 1, 2 * width), F32),
        vmem((2, feats, width), F32),
        vmem((2, feats, width), TRAVEL),
        vmem((2, feats, width), TRAVEL),
        vmem((2, feats, width), TRAVEL),
        vmem((2, feats, width // 2), F32),
        vmem((2, feats, width // 2), TRAVEL),
        vmem((2, feats, width // 2), TRAVEL),
        vmem((2, feats, width // 2), TRAVEL),
        pltpu.SemaphoreType.DMA((24,)),
        pltpu.SemaphoreType.DMA((24,)),
    ]
    summed = pl.pallas_call(
        functools.partial(kernel, peers),
        out_shape=(
            jax.ShapeDtypeStruct((nodes, width), BF),
            jax.ShapeDtypeStruct((2, feats, width), TRAVEL),
            jax.ShapeDtypeStruct((2, feats, width // 2), TRAVEL),
            jax.ShapeDtypeStruct((1, 2 * width), F32),
        ),
        in_specs=[pl.BlockSpec(memory_space=pltpu.HBM)] * 14,
        out_specs=[pl.BlockSpec(memory_space=pltpu.HBM)] * 4,
        scratch_shapes=scratch,
        compiler_params=pltpu.CompilerParams(
            collective_id=0, has_side_effects=True, vmem_limit_bytes=60 * 2**20
        ),
    )(*arguments)
    results = pl.pallas_call(
        finish,
        out_shape=(
            jax.ShapeDtypeStruct((nodes, width), BF),
            jax.ShapeDtypeStruct((feats, width), F32),
            jax.ShapeDtypeStruct((feats, width), F32),
            jax.ShapeDtypeStruct((1, width), F32),
            jax.ShapeDtypeStruct((width, width), F32),
            jax.ShapeDtypeStruct((width, width), F32),
            jax.ShapeDtypeStruct((1, width), F32),
        ),
        in_specs=[pl.BlockSpec(memory_space=pltpu.HBM)] * 4,
        out_specs=[pl.BlockSpec(memory_space=pltpu.HBM)] * 7,
        scratch_shapes=[
            vmem((nodes, width), BF),
            vmem((2, feats, width), TRAVEL),
            vmem((2, feats, width // 2), TRAVEL),
            vmem((1, 2 * width), F32),
            vmem((feats, width), F32),
            vmem((feats, width), F32),
            vmem((width, width), F32),
            vmem((width, width), F32),
            pltpu.SemaphoreType.DMA((11,)),
        ],
        compiler_params=pltpu.CompilerParams(vmem_limit_bytes=60 * 2**20),
    )(*summed)
    return (
        results[0],
        results[1],
        results[2],
        results[3].reshape(width),
        results[4],
        results[5],
        results[6].reshape(width),
    )


def solution(mesh):
    in_specs = (
        P(("dp", "coop"), None),
        P(),
        P(),
        P(),
        P(),
        P(),
        P(),
        P(("dp", "coop"), None, None),
        P(("dp", "coop"), None),
        P(("dp", "coop"), None, None),
        P(("dp", "coop"), None),
        P(("dp", "coop"), None, None),
        P(("dp", "coop")),
        P(("dp", "coop")),
    )
    out_specs = (
        P(("dp", "coop"), None),
        P("dp", None),
        P("dp", None),
        P("dp"),
        P("dp", None),
        P("dp", None),
        P("dp"),
    )
    return jax.shard_map(
        per_device, mesh=mesh, in_specs=in_specs, out_specs=out_specs, check_vma=False
    )
```

```python
import functools

import jax
import jax.numpy as jnp
from jax import lax
from jax.experimental import pallas as pl
from jax.experimental.pallas import tpu as pltpu
from jax.sharding import PartitionSpec as P

MESH = pl.DeviceIdType.MESH
BF = jnp.bfloat16
F32 = jnp.float32
CHUNK = 256
XS = 4
ZS = 8
TRAVEL = jnp.bfloat16
LOAD_ORDER = (7, 9, 11, 0, 2, 8, 10, 12, 13, 1, 3, 4, 5, 6)


def far_x(i):
    return (1 - i // 2) * (2 + i) + (i // 2) * (3 - i)


def far_z(j):
    return ZS // 2 + (j // 2) * (1 - 2 * (j % 2)) - j % 2


def every(body):
    def one(n, carry):
        body(far_x(n // ZS), far_z(n % ZS))
        return carry

    lax.fori_loop(0, XS * ZS, one, 0)


def nn(a, b):
    return lax.dot_general(a, b, (((1,), (0,)), ((), ())), preferred_element_type=F32)


def nt(a, b):
    return lax.dot_general(a, b, (((1,), (1,)), ((), ())), preferred_element_type=F32)


def split(value):
    high = value.astype(BF)
    low = (value - high.astype(F32)).astype(BF)
    return high, low


def blocks(total, step, body):
    def one(i, carry):
        body(pl.ds(pl.multiple_of(i * step, step), step), i * step)
        return carry

    lax.fori_loop(0, total // step, one, 0)


def one_if(flag):
    return jnp.where(flag, 1.0, 0.0).astype(BF)


def kernel(
    peers,
    *refs,
):
    arguments, refs = refs[:14], refs[14:]
    held, refs = refs[4:18], refs[:4] + refs[18:]
    step_through(peers, arguments, held, *refs)


def step_through(
    peers,
    arguments,
    held,
    out_embedding,
    out_one,
    out_two,
    out_bias,
    embedding,
    bias_total,
    out_sems,
    held_sems,
    ask_send,
    ask_recv,
    asked,
    a1,
    a1t,
    a2,
    a2t,
    p1t,
    p2,
    p2t,
    p3,
    p3t,
    source_t,
    source,
    target_t,
    target,
    features_t,
    hidden_t,
    inv1,
    inv2,
    base,
    before,
    hidden,
    left,
    grad,
    own,
    coefs,
    totals,
    sends,
    recvs,
    highs,
    lows,
    bias_send,
    bias_near,
    bias_held,
    bias_recv,
    grads_one,
    pair_one,
    shards_one,
    final_one,
    lines,
    grads_two,
    pair_two,
    shards_two,
    final_two,
    send_sems,
    recv_sems,
    group_sems,
    partial,
    pieces,
):
    me = lax.axis_index("coop")
    chip = me // 2
    core = me % 2
    chips = peers // 2
    barrier = pltpu.get_barrier_semaphore()

    def chip_at(x, z):
        return (chip // ZS + x) % XS * ZS + (chip + z) % ZS

    def to_all(start):
        def both(x, z):
            to = chip_at(x, z) * 2
            start(to + 1 - core)

            @pl.when(to + core != me)
            def _():
                start(to + core)

        every(both)

    def to_others(start):
        def one(x, z):
            to = chip_at(x, z)

            @pl.when(to != chip)
            def _():
                start(to)

        every(one)

    def greet(peer):
        pl.semaphore_signal(barrier, inc=1, device_id={"coop": peer}, device_id_type=MESH)

    to_all(greet)
    loads = [
        pltpu.make_async_copy(argument, place, held_sems.at[n])
        for n, (argument, place) in enumerate(zip(arguments, held))
    ]
    for n in LOAD_ORDER:
        loads[n].start()
    (
        features,
        self_first,
        neighbour_first,
        bias_first,
        self_second,
        neighbour_second,
        bias_second,
        request_first,
        adjacent_first,
        request_second,
        adjacent_second,
        request_edges,
        edge_source,
        edge_target,
    ) = held
    nodes, width = hidden.shape
    feats = features.shape[1]
    slots = a1.shape[1]
    edges = edge_source.shape[1]
    cap = slots // peers
    step = slots // XS

    def count(adjacent, matrix_t):
        tall = 32
        table = adjacent[...]

        def fill(rows, start):
            slot = lax.broadcasted_iota(jnp.int32, (tall, nodes), 0) + start
            total = jnp.zeros((tall, nodes), F32)
            for j in range(table.shape[0]):
                total = total + jnp.where(table[j : j + 1, :] == slot, 1.0, 0.0)
            matrix_t[rows, :] = total.astype(BF)

        blocks(slots, tall, fill)

    def transpose(src, dst):
        def one(rows, start):
            shape = (128, src.shape[1])
            row = lax.broadcasted_iota(jnp.int32, shape, 0) + start
            dst[rows, :] = nt(
                one_if(row == lax.broadcasted_iota(jnp.int32, shape, 1)), src[...]
            ).astype(BF)

        blocks(src.shape[1], 128, one)

    def inverse(matrix, result):
        def one(rows, start):
            result[rows, :] = 1.0 / nn(matrix[rows, :], jnp.ones((slots, width), BF))

        blocks(nodes, CHUNK, one)

    for n in LOAD_ORDER[:5]:
        loads[n].wait()
    for n, request in enumerate((request_first, request_second, request_edges)):
        wanted = request[...].T
        for d in range(peers):
            ask_send[d, :, cap * n : cap * (n + 1)] = wanted[d : d + 1, :]

    def project_first(rows, start):
        left[rows, :] = nn(features[rows, :], neighbour_first[...]).astype(BF)

    blocks(nodes, CHUNK, project_first)
    for n in LOAD_ORDER[5:]:
        loads[n].wait()

    pl.semaphore_wait(barrier, peers - 1)

    def ask(peer):
        pltpu.make_async_remote_copy(
            ask_send.at[peer],
            ask_recv.at[me],
            send_sems.at[15],
            recv_sems.at[15],
            device_id={"coop": peer},
            device_id_type=MESH,
        ).start()

    to_all(ask)
    ask_recv[pl.ds(me, 1)] = ask_send[pl.ds(me, 1)]

    def base_first(rows, start):
        base[rows, :] = nn(features[rows, :], self_first[...]) + bias_first[...]

    blocks(nodes, CHUNK, base_first)
    count(adjacent_first, a1t)

    others = pl.ds(0, peers - 1)
    pltpu.make_async_copy(ask_recv.at[others], ask_recv.at[others], recv_sems.at[15]).wait()
    for d in range(peers):
        asked[d : d + 1, :] = ask_recv[d]

    def mine(n, start):
        table = asked[...]
        low = table % 16
        parts = jnp.concatenate([table - low, low], axis=1).astype(F32).astype(BF)
        row = lax.broadcasted_iota(jnp.int32, (step, peers), 0) + start
        owner = lax.broadcasted_iota(jnp.int32, (step, peers), 1)
        spread = nn(one_if(row // cap == owner), parts)
        row = lax.broadcasted_iota(jnp.int32, spread.shape, 0) + start
        lane = lax.broadcasted_iota(jnp.int32, spread.shape, 1) % 128
        return jnp.where(lane == n * cap + row % cap, spread, 0.0).astype(BF)

    def picks_of(n, start):
        part = mine(n, start)
        wanted = nt(part, jnp.ones((nodes, part.shape[1]), BF))
        return one_if(wanted == lax.broadcasted_iota(jnp.int32, wanted.shape, 1).astype(F32))

    def picks(n, matrix):
        def one(rows, start):
            matrix[rows, :] = picks_of(n, start)

        blocks(slots, step, one)

    def picks_t(n, matrix):
        def one(rows, start):
            part = mine(n, start)
            wanted = nt(jnp.ones((nodes, part.shape[1]), BF), part)
            matrix[:, rows] = one_if(
                wanted == lax.broadcasted_iota(jnp.int32, wanted.shape, 0).astype(F32)
            )

        blocks(slots, step, one)

    def block(phase, side, peer, dx):
        return pltpu.make_async_remote_copy(
            sends.at[phase, side, pl.ds(pl.multiple_of(peer * cap, cap), cap)],
            recvs.at[phase, side, pl.ds(pl.multiple_of(me * cap, cap), cap)],
            send_sems.at[2 * phase + side],
            group_sems.at[XS * (2 * phase + side) + dx],
            device_id={"coop": peer},
            device_id_type=MESH,
        )

    group = 2 * ZS

    def ship(phase, side, body):
        def one(i, carry):
            x = (chip // ZS + far_x(i)) % XS
            start = x * step
            if body is not None:
                body(pl.ds(pl.multiple_of(start, step), step), start)

            def send(j, carry):
                to = x * group + (chip + far_z(j)) % ZS * 2
                block(phase, side, to + 1 - core, far_x(i)).start()

                @pl.when(to + core != me)
                def _():
                    block(phase, side, to + core, far_x(i)).start()

                return carry

            lax.fori_loop(0, ZS, send, 0)
            return carry

        lax.fori_loop(0, XS, one, 0)
        mine = pl.ds(pl.multiple_of(me * cap, cap), cap)
        recvs[phase, side, mine, :] = sends[phase, side, mine, :]

    def sent(phase, side):
        most = sends.at[phase, side, pl.ds(0, (peers - 1) * cap)]
        pltpu.make_async_copy(most, most, send_sems.at[2 * phase + side]).wait()

    def collect(phase, side, matrix, body):
        for n in range(XS):
            dx = (2, 3, 1, 0)[n]
            count = (group if dx else group - 1) * cap
            some = recvs.at[phase, side, pl.ds(0, count)]
            pltpu.make_async_copy(
                some, some, group_sems.at[XS * (2 * phase + side) + dx]
            ).wait()
            start = (chip // ZS + XS - dx) % XS * step
            slots_there = pl.ds(pl.multiple_of(start, step), step)

            def one(rows, start):
                value = nn(matrix[rows, slots_there], recvs[phase, side, slots_there, :])
                if n:
                    value = value + partial[rows, :]
                if n < XS - 1:
                    partial[rows, :] = value
                else:
                    body(rows, start, value)

            blocks(matrix.shape[0], CHUNK, one)

    half = width // 2
    sides = (slice(0, half), slice(half, width))

    def fill(phase, matrix, rows_of):
        def one(rows, start):
            part = nn(matrix[rows, :], rows_of[...]).astype(BF)
            for side in range(2):
                sends[phase, side, rows, :] = part[:, sides[side]]

        ship(phase, 0, one)
        ship(phase, 1, None)

    def fill_side(phase, side, matrix, rows_of):
        def one(rows, start):
            sends[phase, side, rows, :] = nn(matrix[rows, :], rows_of).astype(BF)

        ship(phase, side, one)

    def joined(value):
        return jnp.concatenate(split(value), axis=1)

    def folded(value):
        return value[:, :half] + value[:, half:]

    def fill_split(phase, side, matrix, value):
        pieces = joined(value)

        def one(rows, start):
            sends[phase, side, rows, :] = folded(nn(matrix[rows, :], pieces)).astype(BF)

        ship(phase, side, one)

    def gather_first(rows, start):
        part = nn(picks_of(0, start), left[...]).astype(BF)
        for side in range(2):
            sends[0, side, rows, :] = part[:, sides[side]]

    ship(0, 0, gather_first)
    ship(0, 1, None)
    transpose(a1t, a1)
    inverse(a1, inv1)
    picks(1, p2)
    count(adjacent_second, a2t)
    picks(2, p3)
    for side in range(2):
        cols = sides[side]

        def layer_one(rows, start, total):
            value = base[rows, cols] + total * inv1[rows, cols]
            before[rows, cols] = value
            part = jnp.maximum(value, 0.0).astype(BF)
            hidden[rows, cols] = part
            more = nn(part, neighbour_second[cols, :])
            if side == 0:
                totals[rows, :] = more
            else:
                left[rows, :] = (totals[rows, :] + more).astype(BF)

        collect(0, side, a1, layer_one)

    fill(1, p2, left)

    def second_base(rows, start):
        base[rows, :] = nn(hidden[rows, :], self_second[...]) + bias_second[...]

    blocks(nodes, CHUNK, second_base)
    transpose(a2t, a2)
    inverse(a2, inv2)
    vertex = lax.broadcasted_iota(jnp.int32, (nodes, edges), 0)
    source_t[...] = one_if(vertex == edge_source[...])
    slot = lax.broadcasted_iota(jnp.int32, (slots, edges), 0)
    target_t[...] = one_if(slot == edge_target[...])
    transpose(source_t, source)
    transpose(target_t, target)
    transpose(hidden, hidden_t)
    for side in range(2):
        cols = sides[side]

        def layer_two(rows, start, total):
            embedding[rows, cols] = (base[rows, cols] + total * inv2[rows, cols]).astype(BF)

        collect(1, side, a2, layer_two)
        fill_side(2, side, p3, embedding[:, cols])
    leave = [
        pltpu.make_async_copy(embedding, out_embedding, out_sems.at[0]),
        pltpu.make_async_copy(bias_total, out_bias, out_sems.at[1]),
        pltpu.make_async_copy(final_one, out_one, out_sems.at[2]),
        pltpu.make_async_copy(final_two, out_two, out_sems.at[3]),
    ]
    leave[0].start()

    def lefts(rows, start):
        left[rows, :] = nn(source[rows, :], embedding[...]).astype(BF)

    blocks(edges, CHUNK, lefts)
    picks_t(2, p3t)
    transpose(features, features_t)
    picks_t(1, p2t)

    def first_scores(rows, start, right):
        own[rows, sides[0]] = right
        grad[rows, sides[0]] = left[rows, sides[0]].astype(F32) * right

    collect(2, 0, target, first_scores)

    def scores(rows, start, right):
        here = left[rows, :].astype(F32)
        products = grad[rows, sides[0]] + here[:, sides[1]] * right
        score = jnp.sum(products, axis=1, keepdims=True) * width ** (-0.5)
        edge = lax.broadcasted_iota(jnp.int32, score.shape, 0) + start
        label = jnp.where(edge < edges // 2, 1.0, 0.0)
        coef = (jax.nn.sigmoid(score) - label) * (edges * peers * width) ** (-0.5)
        grad[rows, :] = coef * here
        own[rows, sides[1]] = right
        coefs[rows, :] = coef

    collect(2, 1, target, scores)
    for side in range(2):
        fill_split(3, side, target_t, grad[:, sides[side]])
    high, low = split(coefs[...] * own[...])
    totals[...] = nn(source_t[...], high) + nn(source_t[...], low)
    picks_t(0, p1t)
    for side in range(2):
        cols = sides[side]

        def outer(rows, start, total):
            grad[rows, cols] = totals[rows, cols] + total

        collect(3, side, p3t, outer)
        fill_split(4, side, a2t, grad[:, cols] * inv2[:, cols])
    bias_send[:, :, :width] = jnp.sum(grad[...], axis=0, keepdims=True)[None]
    outer_round = grad[...].astype(BF)
    grads_one[1, :width, :] = nn(hidden_t[...], outer_round)
    own[...] = nt(outer_round, self_second[...])
    for side in range(2):
        cols = sides[side]
        weight = neighbour_second[:, cols]
        weights = jnp.concatenate([weight, weight], axis=1)

        def second_totals(rows, start, total):
            high, low = split(total)
            highs[rows, cols] = high
            lows[rows, cols] = low
            value = own[rows, :] + nt(jnp.concatenate([high, low], axis=1), weights)
            if side == 0:
                own[rows, :] = value
            else:
                grad[rows, :] = jnp.where(before[rows, :] > 0.0, value, 0.0)

        collect(4, side, p2t, second_totals)

    fill_split(5, 0, a1t, grad[:, sides[0]] * inv1[:, sides[0]])
    inner_round = grad[...].astype(BF)

    def self_gradient(rows, start):
        grads_one[0, rows, :] = nn(features_t[rows, :], inner_round)

    blocks(feats, CHUNK, self_gradient)
    grads_one[1, width:, :] = nn(hidden_t[...], highs[...]) + nn(hidden_t[...], lows[...])

    share = feats // chips
    place = pl.ds(pl.multiple_of(chip * share, share), share)
    partner = chip * 2 + 1 - core

    def to_partner(src, dst, sem):
        return pltpu.make_async_remote_copy(
            src,
            dst,
            send_sems.at[sem],
            recv_sems.at[sem],
            device_id={"coop": partner},
            device_id_type=MESH,
        )

    def send_rows(src, dst, sem, to):
        pltpu.make_async_remote_copy(
            src,
            dst,
            send_sems.at[sem],
            recv_sems.at[sem],
            device_id={"coop": to * 2 + core},
            device_id_type=MESH,
        ).start()

    def to_x(start):
        for dx in (2, 1, 3):
            start((chip // ZS + dx) % XS)

    def to_z(start):
        for dz in (4, 3, 5, 2, 6, 1, 7):
            start((chip % ZS + dz) % ZS)

    def await_rows(ref, count, sem):
        rows = ref.at[pl.ds(0, count)]
        pltpu.make_async_copy(rows, rows, sem).wait()

    my_x, my_z = chip // ZS, chip % ZS
    tall = ZS * share
    x_rows = lambda x: pl.ds(pl.multiple_of(x * tall, tall), tall)
    z_rows = lambda z: pl.ds(pl.multiple_of(z * share, share), share)

    def summed(ref, count, rows):
        total = ref[0:rows, :].astype(F32)
        for c in range(1, count):
            total = total + ref[c * rows : (c + 1) * rows, :].astype(F32)
        return total

    one_swap = to_partner(pair_one.at[0], pair_one.at[1], 16)
    one_back = to_partner(final_one.at[core], final_one.at[core], 17)
    x_send, x_recv = shards_one.at[0], shards_one.at[1]
    z_send, z_recv = lines.at[0], lines.at[1]
    final_mine = final_one.at[core]

    def one_along_x():
        one_swap.wait_recv()
        x_send[...] = (grads_one[core] + pair_one[1].astype(F32)).astype(TRAVEL)
        to_x(lambda x: send_rows(x_send.at[x_rows(x)], x_recv.at[x_rows(my_x)], 18, x * ZS + my_z))
        x_recv[x_rows(my_x), :] = x_send[x_rows(my_x), :]

    def one_along_z():
        await_rows(x_recv, (XS - 1) * tall, recv_sems.at[18])
        z_send[...] = summed(x_recv, XS, tall).astype(TRAVEL)
        to_z(lambda z: send_rows(z_send.at[z_rows(z)], z_recv.at[z_rows(my_z)], 19, my_x * ZS + z))
        z_recv[z_rows(my_z), :] = z_send[z_rows(my_z), :]

    def one_gather_z():
        await_rows(z_recv, (ZS - 1) * share, recv_sems.at[19])
        final_one[core, place, :] = summed(z_recv, ZS, share).astype(TRAVEL)
        here = final_mine.at[place]
        to_z(lambda z: send_rows(here, here, 20, my_x * ZS + z))

    def one_gather_x():
        await_rows(z_recv, (ZS - 1) * share, recv_sems.at[20])
        here = final_mine.at[x_rows(my_x)]
        to_x(lambda x: send_rows(here, here, 21, x * ZS + my_z))

    def one_give_back():
        await_rows(x_recv, (XS - 1) * tall, recv_sems.at[21])
        one_back.start()

    two_swap = to_partner(pair_two.at[0], pair_two.at[1], 22)
    two_back = to_partner(final_two.at[core], final_two.at[core], 23)
    two_send, two_recv = shards_two.at[0], shards_two.at[1]

    def two_swap_side(side):
        @pl.when(core != side)
        def _():
            pair_two[0] = grads_two[side].astype(TRAVEL)
            two_swap.start()

        @pl.when(core == side)
        def _():
            two_swap.wait_recv()
            two_send[...] = (grads_two[side] + pair_two[1].astype(F32)).astype(TRAVEL)
            to_others(
                lambda to: send_rows(
                    two_send.at[pl.ds(pl.multiple_of(to * share, share), share)],
                    two_recv.at[place],
                    12,
                    to,
                )
            )
            two_recv[place, :] = two_send[place, :]

    def two_gather():
        await_rows(two_recv, (chips - 1) * share, recv_sems.at[12])
        final_two[core, place, :] = summed(two_recv, chips, share).astype(TRAVEL)
        here = final_two.at[core, place]
        to_others(lambda to: send_rows(here, here, 24, to))

    def two_give_back():
        await_rows(two_recv, (chips - 1) * share, recv_sems.at[24])
        two_back.start()

    pair_one[0] = grads_one[1 - core].astype(TRAVEL)
    one_swap.start()
    bias_send[:, :, width:] = jnp.sum(grad[...], axis=0, keepdims=True)[None]
    bias_pair = to_partner(bias_send, bias_near, 13)
    bias_pair.start()
    one_along_x()
    fill_split(5, 1, a1t, grad[:, sides[1]] * inv1[:, sides[1]])
    bias_pair.wait_recv()
    bias_held[...] = bias_send[...] + bias_near[...]
    to_others(lambda to: send_rows(bias_held.at[0], bias_recv.at[chip], 14, to))
    bias_recv[pl.ds(chip, 1)] = bias_held[...]

    def near(side):
        def first_totals(rows, start, total):
            pieces[rows, :] = joined(total)

        collect(5, side, p1t, first_totals)

        def near_gradient(rows, start):
            grads_two[side, rows, :] = folded(nn(features_t[rows, :], pieces[...]))

        blocks(feats, CHUNK, near_gradient)
        two_swap_side(side)

    near(0)
    one_along_z()
    near(1)
    one_gather_z()
    far = pl.ds(0, chips - 1)
    pltpu.make_async_copy(bias_recv.at[far], bias_recv.at[far], recv_sems.at[14]).wait()
    total = bias_recv[0]
    for c in range(1, chips):
        total = total + bias_recv[c]
    bias_total[...] = total
    leave[1].start()
    one_gather_x()
    two_gather()
    one_give_back()
    two_give_back()
    one_back.wait_recv()
    leave[2].start()
    two_back.wait_recv()
    leave[3].start()

    pltpu.make_async_copy(ask_send.at[others], ask_send.at[others], send_sems.at[15]).wait()
    for phase in range(6):
        sent(phase, 0)
        sent(phase, 1)
    bias_pair.wait_send()
    pltpu.make_async_copy(bias_recv.at[far], bias_recv.at[far], send_sems.at[14]).wait()
    one_swap.wait_send()
    await_rows(x_recv, (XS - 1) * tall, send_sems.at[18])
    await_rows(z_recv, (ZS - 1) * share, send_sems.at[19])
    await_rows(z_recv, (ZS - 1) * share, send_sems.at[20])
    await_rows(x_recv, (XS - 1) * tall, send_sems.at[21])
    one_back.wait_send()
    two_swap.wait_send()
    await_rows(two_recv, (chips - 1) * share, send_sems.at[12])
    await_rows(two_recv, (chips - 1) * share, send_sems.at[24])
    two_back.wait_send()
    for copy in leave:
        copy.wait()


def finish(
    in_embedding,
    in_one,
    in_two,
    in_bias,
    out_embedding,
    out_self_first,
    out_neighbour_first,
    out_bias_first,
    out_self_second,
    out_neighbour_second,
    out_bias_second,
    embedding,
    one,
    two,
    bias,
    self_first,
    neighbour_first,
    self_second,
    neighbour_second,
    sems,
):
    loads = [
        pltpu.make_async_copy(src, dst, sems.at[7 + n])
        for n, (src, dst) in enumerate(
            ((in_one, one), (in_two, two), (in_embedding, embedding), (in_bias, bias))
        )
    ]
    for load in loads:
        load.start()
    width = embedding.shape[1]
    half = width // 2
    copies = []

    def leave(src, dst):
        copies.append(pltpu.make_async_copy(src, dst, sems.at[len(copies)]))
        copies[-1].start()

    loads[0].wait()
    self_first[...] = one[0].astype(F32)
    leave(self_first, out_self_first)
    loads[1].wait()
    neighbour_first[:, :half] = two[0].astype(F32)
    neighbour_first[:, half:] = two[1].astype(F32)
    leave(neighbour_first, out_neighbour_first)
    loads[2].wait()
    leave(embedding, out_embedding)
    self_second[...] = one[1, :width].astype(F32)
    leave(self_second, out_self_second)
    neighbour_second[...] = one[1, width:].astype(F32)
    leave(neighbour_second, out_neighbour_second)
    loads[3].wait()
    leave(bias.at[:, :width], out_bias_second)
    leave(bias.at[:, width:], out_bias_first)
    for copy in copies:
        copy.wait()


def per_device(
    features,
    self_first,
    neighbour_first,
    bias_first,
    self_second,
    neighbour_second,
    bias_second,
    request_first,
    adjacent_first,
    request_second,
    adjacent_second,
    request_edges,
    edge_source,
    edge_target,
):
    nodes, feats = features.shape
    width = self_first.shape[1]
    _, peers, cap = request_first.shape
    slots = peers * cap
    edges = edge_source.shape[0]
    arguments = (
        features,
        self_first,
        neighbour_first,
        bias_first.reshape(1, width),
        self_second,
        neighbour_second,
        bias_second.reshape(1, width),
        request_first[0].T,
        adjacent_first.T,
        request_second[0].T,
        adjacent_second.T,
        request_edges[0].T,
        edge_source.reshape(1, edges),
        edge_target.reshape(1, edges),
    )
    vmem = pltpu.VMEM
    scratch = [vmem(a.shape, a.dtype) for a in arguments] + [
        vmem((nodes, width), BF),
        vmem((1, 2 * width), F32),
        pltpu.SemaphoreType.DMA((4,)),
        pltpu.SemaphoreType.DMA((14,)),
        vmem((peers, 1, 128), jnp.int32),
        vmem((peers, 1, 128), jnp.int32),
        vmem((peers, 128), jnp.int32),
        vmem((nodes, slots), BF),
        vmem((slots, nodes), BF),
        vmem((nodes, slots), BF),
        vmem((slots, nodes), BF),
        vmem((nodes, slots), BF),
        vmem((slots, nodes), BF),
        vmem((nodes, slots), BF),
        vmem((slots, nodes), BF),
        vmem((nodes, slots), BF),
        vmem((nodes, edges), BF),
        vmem((edges, nodes), BF),
        vmem((slots, edges), BF),
        vmem((edges, slots), BF),
        vmem((feats, nodes), BF),
        vmem((width, nodes), BF),
        vmem((nodes, width), F32),
        vmem((nodes, width), F32),
        vmem((nodes, width), F32),
        vmem((nodes, width), F32),
        vmem((nodes, width), BF),
        vmem((nodes, width), BF),
        vmem((nodes, width), F32),
        vmem((nodes, width), F32),
        vmem((edges, 1), F32),
        vmem((nodes, width), F32),
        vmem((6, 2, slots, width // 2), BF),
        vmem((6, 2, slots, width // 2), BF),
        vmem((nodes, width), BF),
        vmem((nodes, width), BF),
        vmem((1, 1, 2 * width), F32),
        vmem((1, 1, 2 * width), F32),
        vmem((1, 1, 2 * width), F32),
        vmem((peers // 2, 1, 2 * width), F32),
        vmem((2, feats, width), F32),
        vmem((2, feats, width), TRAVEL),
        vmem((2, feats, width), TRAVEL),
        vmem((2, feats, width), TRAVEL),
        vmem((2, feats // XS, width), TRAVEL),
        vmem((2, feats, width // 2), F32),
        vmem((2, feats, width // 2), TRAVEL),
        vmem((2, feats, width // 2), TRAVEL),
        vmem((2, feats, width // 2), TRAVEL),
        pltpu.SemaphoreType.DMA((25,)),
        pltpu.SemaphoreType.DMA((25,)),
        pltpu.SemaphoreType.DMA((12 * XS,)),
        vmem((nodes, width // 2), F32),
        vmem((nodes, width), BF),
    ]
    summed = pl.pallas_call(
        functools.partial(kernel, peers),
        out_shape=(
            jax.ShapeDtypeStruct((nodes, width), BF),
            jax.ShapeDtypeStruct((2, feats, width), TRAVEL),
            jax.ShapeDtypeStruct((2, feats, width // 2), TRAVEL),
            jax.ShapeDtypeStruct((1, 2 * width), F32),
        ),
        in_specs=[pl.BlockSpec(memory_space=pltpu.HBM)] * 14,
        out_specs=[pl.BlockSpec(memory_space=pltpu.HBM)] * 4,
        scratch_shapes=scratch,
        compiler_params=pltpu.CompilerParams(
            collective_id=0, has_side_effects=True, vmem_limit_bytes=60 * 2**20
        ),
    )(*arguments)
    results = pl.pallas_call(
        finish,
        out_shape=(
            jax.ShapeDtypeStruct((nodes, width), BF),
            jax.ShapeDtypeStruct((feats, width), F32),
            jax.ShapeDtypeStruct((feats, width), F32),
            jax.ShapeDtypeStruct((1, width), F32),
            jax.ShapeDtypeStruct((width, width), F32),
            jax.ShapeDtypeStruct((width, width), F32),
            jax.ShapeDtypeStruct((1, width), F32),
        ),
        in_specs=[pl.BlockSpec(memory_space=pltpu.HBM)] * 4,
        out_specs=[pl.BlockSpec(memory_space=pltpu.HBM)] * 7,
        scratch_shapes=[
            vmem((nodes, width), BF),
            vmem((2, feats, width), TRAVEL),
            vmem((2, feats, width // 2), TRAVEL),
            vmem((1, 2 * width), F32),
            vmem((feats, width), F32),
            vmem((feats, width), F32),
            vmem((width, width), F32),
            vmem((width, width), F32),
            pltpu.SemaphoreType.DMA((11,)),
        ],
        compiler_params=pltpu.CompilerParams(vmem_limit_bytes=60 * 2**20),
    )(*summed)
    return (
        results[0],
        results[1],
        results[2],
        results[3].reshape(width),
        results[4],
        results[5],
        results[6].reshape(width),
    )


def solution(mesh):
    in_specs = (
        P(("dp", "coop"), None),
        P(),
        P(),
        P(),
        P(),
        P(),
        P(),
        P(("dp", "coop"), None, None),
        P(("dp", "coop"), None),
        P(("dp", "coop"), None, None),
        P(("dp", "coop"), None),
        P(("dp", "coop"), None, None),
        P(("dp", "coop")),
        P(("dp", "coop")),
    )
    out_specs = (
        P(("dp", "coop"), None),
        P("dp", None),
        P("dp", None),
        P("dp"),
        P("dp", None),
        P("dp", None),
        P("dp"),
    )
    return jax.shard_map(
        per_device, mesh=mesh, in_specs=in_specs, out_specs=out_specs, check_vma=False
    )
```

```python
import functools

import jax
import jax.numpy as jnp
from jax import lax
from jax.experimental import pallas as pl
from jax.experimental.pallas import tpu as pltpu
from jax.sharding import PartitionSpec as P

MESH = pl.DeviceIdType.MESH
BF = jnp.bfloat16
F32 = jnp.float32
CHUNK = 256
XS = 4
ZS = 8
TRAVEL = jnp.bfloat16
LOAD_ORDER = (7, 9, 11, 0, 2, 8, 10, 12, 13, 1, 3, 4, 5, 6)


def far_x(i):
    return (1 - i // 2) * (2 + i) + (i // 2) * (3 - i)


def far_z(j):
    return ZS // 2 + (j // 2) * (1 - 2 * (j % 2)) - j % 2


def every(body):
    def one(n, carry):
        body(far_x(n // ZS), far_z(n % ZS))
        return carry

    lax.fori_loop(0, XS * ZS, one, 0, unroll=ZS)


def nn(a, b):
    return lax.dot_general(a, b, (((1,), (0,)), ((), ())), preferred_element_type=F32)


def nt(a, b):
    return lax.dot_general(a, b, (((1,), (1,)), ((), ())), preferred_element_type=F32)


def split(value):
    high = value.astype(BF)
    low = (value - high.astype(F32)).astype(BF)
    return high, low


def blocks(total, step, body):
    def one(i, carry):
        body(pl.ds(pl.multiple_of(i * step, step), step), i * step)
        return carry

    lax.fori_loop(0, total // step, one, 0)


def one_if(flag):
    return jnp.where(flag, 1.0, 0.0).astype(BF)


def kernel(
    peers,
    *refs,
):
    arguments, refs = refs[:14], refs[14:]
    held, refs = refs[4:18], refs[:4] + refs[18:]
    step_through(peers, arguments, held, *refs)


def step_through(
    peers,
    arguments,
    held,
    out_embedding,
    out_one,
    out_two,
    out_bias,
    embedding,
    bias_total,
    out_sems,
    held_sems,
    ask_send,
    ask_recv,
    asked,
    a1,
    a1t,
    a2,
    a2t,
    p1t,
    p2,
    p2t,
    p3,
    p3t,
    source_t,
    source,
    target_t,
    target,
    features_t,
    hidden_t,
    inv1,
    inv2,
    base,
    before,
    hidden,
    left,
    grad,
    own,
    coefs,
    totals,
    sends,
    recvs,
    highs,
    lows,
    bias_send,
    bias_near,
    bias_held,
    bias_recv,
    grads_one,
    pair_one,
    shards_one,
    final_one,
    lines,
    grads_two,
    pair_two,
    shards_two,
    final_two,
    send_sems,
    recv_sems,
    group_sems,
    partial,
    pieces,
):
    me = lax.axis_index("coop")
    chip = me // 2
    core = me % 2
    chips = peers // 2
    barrier = pltpu.get_barrier_semaphore()

    def chip_at(x, z):
        return (chip // ZS + x) % XS * ZS + (chip + z) % ZS

    def to_all(start):
        def both(x, z):
            to = chip_at(x, z) * 2
            start(to + 1 - core, x)

            @pl.when(to + core != me)
            def _():
                start(to + core, x)

        every(both)

    def to_others(start):
        def one(x, z):
            to = chip_at(x, z)

            @pl.when(to != chip)
            def _():
                start(to)

        every(one)

    def greet(peer, x):
        pl.semaphore_signal(barrier, inc=1, device_id={"coop": peer}, device_id_type=MESH)

    to_all(greet)
    loads = [
        pltpu.make_async_copy(argument, place, held_sems.at[n])
        for n, (argument, place) in enumerate(zip(arguments, held))
    ]
    for n in LOAD_ORDER:
        loads[n].start()
    (
        features,
        self_first,
        neighbour_first,
        bias_first,
        self_second,
        neighbour_second,
        bias_second,
        request_first,
        adjacent_first,
        request_second,
        adjacent_second,
        request_edges,
        edge_source,
        edge_target,
    ) = held
    nodes, width = hidden.shape
    feats = features.shape[1]
    slots = a1.shape[1]
    edges = edge_source.shape[1]
    cap = slots // peers
    step = slots // XS

    def count(adjacent, matrix_t):
        tall = 32
        table = adjacent[...]

        def fill(rows, start):
            slot = lax.broadcasted_iota(jnp.int32, (tall, nodes), 0) + start
            total = jnp.zeros((tall, nodes), F32)
            for j in range(table.shape[0]):
                total = total + jnp.where(table[j : j + 1, :] == slot, 1.0, 0.0)
            matrix_t[rows, :] = total.astype(BF)

        blocks(slots, tall, fill)

    def transpose(src, dst):
        def one(rows, start):
            shape = (128, src.shape[1])
            row = lax.broadcasted_iota(jnp.int32, shape, 0) + start
            dst[rows, :] = nt(
                one_if(row == lax.broadcasted_iota(jnp.int32, shape, 1)), src[...]
            ).astype(BF)

        blocks(src.shape[1], 128, one)

    def inverse(matrix, result):
        def one(rows, start):
            result[rows, :] = 1.0 / nn(matrix[rows, :], jnp.ones((slots, width), BF))

        blocks(nodes, CHUNK, one)

    for n in LOAD_ORDER[:5]:
        loads[n].wait()
    for n, request in enumerate((request_first, request_second, request_edges)):
        wanted = request[...].T
        for d in range(peers):
            ask_send[d, :, cap * n : cap * (n + 1)] = wanted[d : d + 1, :]

    def project_first(rows, start):
        left[rows, :] = nn(features[rows, :], neighbour_first[...]).astype(BF)

    blocks(nodes, CHUNK, project_first)
    for n in LOAD_ORDER[5:]:
        loads[n].wait()

    pl.semaphore_wait(barrier, peers - 1)

    def ask(peer, x):
        pltpu.make_async_remote_copy(
            ask_send.at[peer],
            ask_recv.at[me],
            send_sems.at[15],
            group_sems.at[12 * XS + x],
            device_id={"coop": peer},
            device_id_type=MESH,
        ).start()

    to_all(ask)
    ask_recv[pl.ds(me, 1)] = ask_send[pl.ds(me, 1)]

    def base_first(rows, start):
        base[rows, :] = nn(features[rows, :], self_first[...]) + bias_first[...]

    blocks(nodes, CHUNK, base_first)
    count(adjacent_first, a1t)

    others = pl.ds(0, peers - 1)
    group = 2 * ZS

    def asks_from(i):
        dx = (XS - (2, 3, 1, 0)[i]) % XS
        some = ask_recv.at[pl.ds(0, group if dx else group - 1)]
        pltpu.make_async_copy(some, some, group_sems.at[12 * XS + dx]).wait()
        first = (chip // ZS + XS - dx) % XS * group
        for d in range(group):
            asked[pl.ds(first + d, 1), :] = ask_recv[first + d]

    def mine(n, start):
        table = asked[pl.ds(pl.multiple_of(start // cap, group), group), :]
        low = table % 16
        parts = jnp.concatenate([table - low, low], axis=1).astype(F32).astype(BF)
        row = lax.broadcasted_iota(jnp.int32, (step, group), 0)
        owner = lax.broadcasted_iota(jnp.int32, (step, group), 1)
        spread = nn(one_if(row // cap == owner), parts)
        row = lax.broadcasted_iota(jnp.int32, spread.shape, 0)
        lane = lax.broadcasted_iota(jnp.int32, spread.shape, 1) % 128
        return jnp.where(lane == n * cap + row % cap, spread, 0.0).astype(BF)

    def picks_of(n, start):
        part = mine(n, start)
        wanted = nt(part, jnp.ones((nodes, part.shape[1]), BF))
        return one_if(wanted == lax.broadcasted_iota(jnp.int32, wanted.shape, 1).astype(F32))

    def picks(n, matrix):
        def one(rows, start):
            matrix[rows, :] = picks_of(n, start)

        blocks(slots, step, one)

    def picks_t(n, matrix):
        def one(rows, start):
            part = mine(n, start)
            wanted = nt(jnp.ones((nodes, part.shape[1]), BF), part)
            matrix[:, rows] = one_if(
                wanted == lax.broadcasted_iota(jnp.int32, wanted.shape, 0).astype(F32)
            )

        blocks(slots, step, one)

    def block(phase, side, peer, dx):
        return pltpu.make_async_remote_copy(
            sends.at[phase, side, pl.ds(pl.multiple_of(peer * cap, cap), cap)],
            recvs.at[phase, side, pl.ds(pl.multiple_of(me * cap, cap), cap)],
            send_sems.at[2 * phase + side],
            group_sems.at[XS * (2 * phase + side) + dx],
            device_id={"coop": peer},
            device_id_type=MESH,
        )

    def ship(phase, side, body, ahead=None):
        def one(i, carry):
            x = (chip // ZS + far_x(i)) % XS
            start = x * step
            if body is not None:
                body(pl.ds(pl.multiple_of(start, step), step), start)

            def send(j, carry):
                to = x * group + (chip + far_z(j)) % ZS * 2
                block(phase, side, to + 1 - core, far_x(i)).start()

                @pl.when(to + core != me)
                def _():
                    block(phase, side, to + core, far_x(i)).start()

                return carry

            lax.fori_loop(0, ZS, send, 0, unroll=True)
            return carry

        if ahead is None:
            lax.fori_loop(0, XS, one, 0)
        else:
            for i in range(XS):
                ahead(i)
                one(i, 0)
        mine = pl.ds(pl.multiple_of(me * cap, cap), cap)
        recvs[phase, side, mine, :] = sends[phase, side, mine, :]

    def sent(phase, side):
        most = sends.at[phase, side, pl.ds(0, (peers - 1) * cap)]
        pltpu.make_async_copy(most, most, send_sems.at[2 * phase + side]).wait()

    def collect(phase, side, matrix, body):
        for n in range(XS):
            dx = (2, 3, 1, 0)[n]
            count = (group if dx else group - 1) * cap
            some = recvs.at[phase, side, pl.ds(0, count)]
            pltpu.make_async_copy(
                some, some, group_sems.at[XS * (2 * phase + side) + dx]
            ).wait()
            start = (chip // ZS + XS - dx) % XS * step
            slots_there = pl.ds(pl.multiple_of(start, step), step)

            def one(rows, start):
                value = nn(matrix[rows, slots_there], recvs[phase, side, slots_there, :])
                if n:
                    value = value + partial[rows, :]
                if n < XS - 1:
                    partial[rows, :] = value
                else:
                    body(rows, start, value)

            blocks(matrix.shape[0], CHUNK, one)

    half = width // 2
    sides = (slice(0, half), slice(half, width))

    def fill(phase, matrix, rows_of):
        def one(rows, start):
            part = nn(matrix[rows, :], rows_of[...]).astype(BF)
            for side in range(2):
                sends[phase, side, rows, :] = part[:, sides[side]]

        ship(phase, 0, one)
        ship(phase, 1, None)

    def fill_side(phase, side, matrix, rows_of):
        def one(rows, start):
            sends[phase, side, rows, :] = nn(matrix[rows, :], rows_of).astype(BF)

        ship(phase, side, one)

    def joined(value):
        return jnp.concatenate(split(value), axis=1)

    def folded(value):
        return value[:, :half] + value[:, half:]

    def fill_split(phase, side, matrix, value):
        pieces = joined(value)

        def one(rows, start):
            sends[phase, side, rows, :] = folded(nn(matrix[rows, :], pieces)).astype(BF)

        ship(phase, side, one)

    def gather_first(rows, start):
        part = nn(picks_of(0, start), left[...]).astype(BF)
        for side in range(2):
            sends[0, side, rows, :] = part[:, sides[side]]

    ship(0, 0, gather_first, asks_from)
    ship(0, 1, None)
    transpose(a1t, a1)
    inverse(a1, inv1)
    picks(1, p2)
    count(adjacent_second, a2t)
    picks(2, p3)
    for side in range(2):
        cols = sides[side]

        def layer_one(rows, start, total):
            value = base[rows, cols] + total * inv1[rows, cols]
            before[rows, cols] = value
            part = jnp.maximum(value, 0.0).astype(BF)
            hidden[rows, cols] = part
            more = nn(part, neighbour_second[cols, :])
            if side == 0:
                totals[rows, :] = more
            else:
                left[rows, :] = (totals[rows, :] + more).astype(BF)

        collect(0, side, a1, layer_one)

    fill(1, p2, left)

    def second_base(rows, start):
        base[rows, :] = nn(hidden[rows, :], self_second[...]) + bias_second[...]

    blocks(nodes, CHUNK, second_base)
    transpose(a2t, a2)
    inverse(a2, inv2)
    vertex = lax.broadcasted_iota(jnp.int32, (nodes, edges), 0)
    source_t[...] = one_if(vertex == edge_source[...])
    slot = lax.broadcasted_iota(jnp.int32, (slots, edges), 0)
    target_t[...] = one_if(slot == edge_target[...])
    transpose(source_t, source)
    transpose(target_t, target)
    transpose(hidden, hidden_t)
    for side in range(2):
        cols = sides[side]

        def layer_two(rows, start, total):
            embedding[rows, cols] = (base[rows, cols] + total * inv2[rows, cols]).astype(BF)

        collect(1, side, a2, layer_two)
        fill_side(2, side, p3, embedding[:, cols])
    leave = [
        pltpu.make_async_copy(embedding, out_embedding, out_sems.at[0]),
        pltpu.make_async_copy(bias_total, out_bias, out_sems.at[1]),
        pltpu.make_async_copy(final_one, out_one, out_sems.at[2]),
        pltpu.make_async_copy(final_two, out_two, out_sems.at[3]),
    ]
    leave[0].start()

    def lefts(rows, start):
        left[rows, :] = nn(source[rows, :], embedding[...]).astype(BF)

    blocks(edges, CHUNK, lefts)
    picks_t(2, p3t)
    transpose(features, features_t)
    picks_t(1, p2t)

    def first_scores(rows, start, right):
        own[rows, sides[0]] = right
        grad[rows, sides[0]] = left[rows, sides[0]].astype(F32) * right

    collect(2, 0, target, first_scores)

    def scores(rows, start, right):
        here = left[rows, :].astype(F32)
        products = grad[rows, sides[0]] + here[:, sides[1]] * right
        score = jnp.sum(products, axis=1, keepdims=True) * width ** (-0.5)
        edge = lax.broadcasted_iota(jnp.int32, score.shape, 0) + start
        label = jnp.where(edge < edges // 2, 1.0, 0.0)
        coef = (jax.nn.sigmoid(score) - label) * (edges * peers * width) ** (-0.5)
        grad[rows, :] = coef * here
        own[rows, sides[1]] = right
        coefs[rows, :] = coef

    collect(2, 1, target, scores)
    for side in range(2):
        fill_split(3, side, target_t, grad[:, sides[side]])
    high, low = split(coefs[...] * own[...])
    totals[...] = nn(source_t[...], high) + nn(source_t[...], low)
    picks_t(0, p1t)
    for side in range(2):
        cols = sides[side]

        def outer(rows, start, total):
            grad[rows, cols] = totals[rows, cols] + total

        collect(3, side, p3t, outer)
        fill_split(4, side, a2t, grad[:, cols] * inv2[:, cols])
    bias_send[:, :, :width] = jnp.sum(grad[...], axis=0, keepdims=True)[None]
    outer_round = grad[...].astype(BF)
    grads_one[1, :width, :] = nn(hidden_t[...], outer_round)
    own[...] = nt(outer_round, self_second[...])
    for side in range(2):
        cols = sides[side]
        weight = neighbour_second[:, cols]
        weights = jnp.concatenate([weight, weight], axis=1)

        def second_totals(rows, start, total):
            high, low = split(total)
            highs[rows, cols] = high
            lows[rows, cols] = low
            value = own[rows, :] + nt(jnp.concatenate([high, low], axis=1), weights)
            if side == 0:
                own[rows, :] = value
            else:
                grad[rows, :] = jnp.where(before[rows, :] > 0.0, value, 0.0)

        collect(4, side, p2t, second_totals)

    fill_split(5, 0, a1t, grad[:, sides[0]] * inv1[:, sides[0]])
    inner_round = grad[...].astype(BF)

    def self_gradient(rows, start):
        grads_one[0, rows, :] = nn(features_t[rows, :], inner_round)

    blocks(feats, CHUNK, self_gradient)
    grads_one[1, width:, :] = nn(hidden_t[...], highs[...]) + nn(hidden_t[...], lows[...])

    share = feats // chips
    place = pl.ds(pl.multiple_of(chip * share, share), share)
    partner = chip * 2 + 1 - core

    def to_partner(src, dst, sem):
        return pltpu.make_async_remote_copy(
            src,
            dst,
            send_sems.at[sem],
            recv_sems.at[sem],
            device_id={"coop": partner},
            device_id_type=MESH,
        )

    def send_rows(src, dst, sem, to):
        pltpu.make_async_remote_copy(
            src,
            dst,
            send_sems.at[sem],
            recv_sems.at[sem],
            device_id={"coop": to * 2 + core},
            device_id_type=MESH,
        ).start()

    def to_x(start):
        for dx in (2, 1, 3):
            start((chip // ZS + dx) % XS)

    def to_z(start):
        for dz in (4, 3, 5, 2, 6, 1, 7):
            start((chip % ZS + dz) % ZS)

    def await_rows(ref, count, sem):
        rows = ref.at[pl.ds(0, count)]
        pltpu.make_async_copy(rows, rows, sem).wait()

    my_x, my_z = chip // ZS, chip % ZS
    tall = ZS * share
    x_rows = lambda x: pl.ds(pl.multiple_of(x * tall, tall), tall)
    z_rows = lambda z: pl.ds(pl.multiple_of(z * share, share), share)

    def summed(ref, count, rows):
        total = ref[0:rows, :].astype(F32)
        for c in range(1, count):
            total = total + ref[c * rows : (c + 1) * rows, :].astype(F32)
        return total

    one_swap = to_partner(pair_one.at[0], pair_one.at[1], 16)
    one_back = to_partner(final_one.at[core], final_one.at[core], 17)
    x_send, x_recv = shards_one.at[0], shards_one.at[1]
    z_send, z_recv = lines.at[0], lines.at[1]
    final_mine = final_one.at[core]

    def one_along_x():
        one_swap.wait_recv()
        x_send[...] = (grads_one[core] + pair_one[1].astype(F32)).astype(TRAVEL)
        to_x(lambda x: send_rows(x_send.at[x_rows(x)], x_recv.at[x_rows(my_x)], 18, x * ZS + my_z))
        x_recv[x_rows(my_x), :] = x_send[x_rows(my_x), :]

    def one_along_z():
        await_rows(x_recv, (XS - 1) * tall, recv_sems.at[18])
        z_send[...] = summed(x_recv, XS, tall).astype(TRAVEL)
        to_z(lambda z: send_rows(z_send.at[z_rows(z)], z_recv.at[z_rows(my_z)], 19, my_x * ZS + z))
        z_recv[z_rows(my_z), :] = z_send[z_rows(my_z), :]

    def one_gather_z():
        await_rows(z_recv, (ZS - 1) * share, recv_sems.at[19])
        final_one[core, place, :] = summed(z_recv, ZS, share).astype(TRAVEL)
        here = final_mine.at[place]
        to_z(lambda z: send_rows(here, here, 20, my_x * ZS + z))

    def one_gather_x():
        await_rows(z_recv, (ZS - 1) * share, recv_sems.at[20])
        here = final_mine.at[x_rows(my_x)]
        to_x(lambda x: send_rows(here, here, 21, x * ZS + my_z))

    def one_give_back():
        await_rows(x_recv, (XS - 1) * tall, recv_sems.at[21])
        one_back.start()

    two_swap = to_partner(pair_two.at[0], pair_two.at[1], 22)
    two_back = to_partner(final_two.at[core], final_two.at[core], 23)
    two_send, two_recv = shards_two.at[0], shards_two.at[1]

    def two_swap_side(side):
        @pl.when(core != side)
        def _():
            pair_two[0] = grads_two[side].astype(TRAVEL)
            two_swap.start()

        @pl.when(core == side)
        def _():
            two_swap.wait_recv()
            two_send[...] = (grads_two[side] + pair_two[1].astype(F32)).astype(TRAVEL)
            to_others(
                lambda to: send_rows(
                    two_send.at[pl.ds(pl.multiple_of(to * share, share), share)],
                    two_recv.at[place],
                    12,
                    to,
                )
            )
            two_recv[place, :] = two_send[place, :]

    def two_gather():
        await_rows(two_recv, (chips - 1) * share, recv_sems.at[12])
        final_two[core, place, :] = summed(two_recv, chips, share).astype(TRAVEL)
        here = final_two.at[core, place]
        to_others(lambda to: send_rows(here, here, 24, to))

    def two_give_back():
        await_rows(two_recv, (chips - 1) * share, recv_sems.at[24])
        two_back.start()

    pair_one[0] = grads_one[1 - core].astype(TRAVEL)
    one_swap.start()
    bias_send[:, :, width:] = jnp.sum(grad[...], axis=0, keepdims=True)[None]
    bias_pair = to_partner(bias_send, bias_near, 13)
    bias_pair.start()
    one_along_x()
    fill_split(5, 1, a1t, grad[:, sides[1]] * inv1[:, sides[1]])
    bias_pair.wait_recv()
    bias_held[...] = bias_send[...] + bias_near[...]
    to_others(lambda to: send_rows(bias_held.at[0], bias_recv.at[chip], 14, to))
    bias_recv[pl.ds(chip, 1)] = bias_held[...]

    def near(side):
        def first_totals(rows, start, total):
            pieces[rows, :] = joined(total)

        collect(5, side, p1t, first_totals)

        def near_gradient(rows, start):
            grads_two[side, rows, :] = folded(nn(features_t[rows, :], pieces[...]))

        blocks(feats, CHUNK, near_gradient)
        two_swap_side(side)

    near(0)
    one_along_z()
    near(1)
    one_gather_z()
    far = pl.ds(0, chips - 1)
    pltpu.make_async_copy(bias_recv.at[far], bias_recv.at[far], recv_sems.at[14]).wait()
    total = bias_recv[0]
    for c in range(1, chips):
        total = total + bias_recv[c]
    bias_total[...] = total
    leave[1].start()
    one_gather_x()
    two_gather()
    one_give_back()
    two_give_back()
    one_back.wait_recv()
    leave[2].start()
    two_back.wait_recv()
    leave[3].start()

    pltpu.make_async_copy(ask_send.at[others], ask_send.at[others], send_sems.at[15]).wait()
    for phase in range(6):
        sent(phase, 0)
        sent(phase, 1)
    bias_pair.wait_send()
    pltpu.make_async_copy(bias_recv.at[far], bias_recv.at[far], send_sems.at[14]).wait()
    one_swap.wait_send()
    await_rows(x_recv, (XS - 1) * tall, send_sems.at[18])
    await_rows(z_recv, (ZS - 1) * share, send_sems.at[19])
    await_rows(z_recv, (ZS - 1) * share, send_sems.at[20])
    await_rows(x_recv, (XS - 1) * tall, send_sems.at[21])
    one_back.wait_send()
    two_swap.wait_send()
    await_rows(two_recv, (chips - 1) * share, send_sems.at[12])
    await_rows(two_recv, (chips - 1) * share, send_sems.at[24])
    two_back.wait_send()
    for copy in leave:
        copy.wait()


def finish(
    in_embedding,
    in_one,
    in_two,
    in_bias,
    out_embedding,
    out_self_first,
    out_neighbour_first,
    out_bias_first,
    out_self_second,
    out_neighbour_second,
    out_bias_second,
    embedding,
    one,
    two,
    bias,
    self_first,
    neighbour_first,
    self_second,
    neighbour_second,
    sems,
):
    loads = [
        pltpu.make_async_copy(src, dst, sems.at[7 + n])
        for n, (src, dst) in enumerate(
            ((in_one, one), (in_two, two), (in_embedding, embedding), (in_bias, bias))
        )
    ]
    for load in loads:
        load.start()
    width = embedding.shape[1]
    half = width // 2
    copies = []

    def leave(src, dst):
        copies.append(pltpu.make_async_copy(src, dst, sems.at[len(copies)]))
        copies[-1].start()

    loads[0].wait()
    self_first[...] = one[0].astype(F32)
    leave(self_first, out_self_first)
    loads[1].wait()
    neighbour_first[:, :half] = two[0].astype(F32)
    neighbour_first[:, half:] = two[1].astype(F32)
    leave(neighbour_first, out_neighbour_first)
    loads[2].wait()
    leave(embedding, out_embedding)
    self_second[...] = one[1, :width].astype(F32)
    leave(self_second, out_self_second)
    neighbour_second[...] = one[1, width:].astype(F32)
    leave(neighbour_second, out_neighbour_second)
    loads[3].wait()
    leave(bias.at[:, :width], out_bias_second)
    leave(bias.at[:, width:], out_bias_first)
    for copy in copies:
        copy.wait()


def per_device(
    features,
    self_first,
    neighbour_first,
    bias_first,
    self_second,
    neighbour_second,
    bias_second,
    request_first,
    adjacent_first,
    request_second,
    adjacent_second,
    request_edges,
    edge_source,
    edge_target,
):
    nodes, feats = features.shape
    width = self_first.shape[1]
    _, peers, cap = request_first.shape
    slots = peers * cap
    edges = edge_source.shape[0]
    arguments = (
        features,
        self_first,
        neighbour_first,
        bias_first.reshape(1, width),
        self_second,
        neighbour_second,
        bias_second.reshape(1, width),
        request_first[0].T,
        adjacent_first.T,
        request_second[0].T,
        adjacent_second.T,
        request_edges[0].T,
        edge_source.reshape(1, edges),
        edge_target.reshape(1, edges),
    )
    vmem = pltpu.VMEM
    scratch = [vmem(a.shape, a.dtype) for a in arguments] + [
        vmem((nodes, width), BF),
        vmem((1, 2 * width), F32),
        pltpu.SemaphoreType.DMA((4,)),
        pltpu.SemaphoreType.DMA((14,)),
        vmem((peers, 1, 128), jnp.int32),
        vmem((peers, 1, 128), jnp.int32),
        vmem((peers, 128), jnp.int32),
        vmem((nodes, slots), BF),
        vmem((slots, nodes), BF),
        vmem((nodes, slots), BF),
        vmem((slots, nodes), BF),
        vmem((nodes, slots), BF),
        vmem((slots, nodes), BF),
        vmem((nodes, slots), BF),
        vmem((slots, nodes), BF),
        vmem((nodes, slots), BF),
        vmem((nodes, edges), BF),
        vmem((edges, nodes), BF),
        vmem((slots, edges), BF),
        vmem((edges, slots), BF),
        vmem((feats, nodes), BF),
        vmem((width, nodes), BF),
        vmem((nodes, width), F32),
        vmem((nodes, width), F32),
        vmem((nodes, width), F32),
        vmem((nodes, width), F32),
        vmem((nodes, width), BF),
        vmem((nodes, width), BF),
        vmem((nodes, width), F32),
        vmem((nodes, width), F32),
        vmem((edges, 1), F32),
        vmem((nodes, width), F32),
        vmem((6, 2, slots, width // 2), BF),
        vmem((6, 2, slots, width // 2), BF),
        vmem((nodes, width), BF),
        vmem((nodes, width), BF),
        vmem((1, 1, 2 * width), F32),
        vmem((1, 1, 2 * width), F32),
        vmem((1, 1, 2 * width), F32),
        vmem((peers // 2, 1, 2 * width), F32),
        vmem((2, feats, width), F32),
        vmem((2, feats, width), TRAVEL),
        vmem((2, feats, width), TRAVEL),
        vmem((2, feats, width), TRAVEL),
        vmem((2, feats // XS, width), TRAVEL),
        vmem((2, feats, width // 2), F32),
        vmem((2, feats, width // 2), TRAVEL),
        vmem((2, feats, width // 2), TRAVEL),
        vmem((2, feats, width // 2), TRAVEL),
        pltpu.SemaphoreType.DMA((25,)),
        pltpu.SemaphoreType.DMA((25,)),
        pltpu.SemaphoreType.DMA((13 * XS,)),
        vmem((nodes, width // 2), F32),
        vmem((nodes, width), BF),
    ]
    summed = pl.pallas_call(
        functools.partial(kernel, peers),
        out_shape=(
            jax.ShapeDtypeStruct((nodes, width), BF),
            jax.ShapeDtypeStruct((2, feats, width), TRAVEL),
            jax.ShapeDtypeStruct((2, feats, width // 2), TRAVEL),
            jax.ShapeDtypeStruct((1, 2 * width), F32),
        ),
        in_specs=[pl.BlockSpec(memory_space=pltpu.HBM)] * 14,
        out_specs=[pl.BlockSpec(memory_space=pltpu.HBM)] * 4,
        scratch_shapes=scratch,
        compiler_params=pltpu.CompilerParams(
            collective_id=0, has_side_effects=True, vmem_limit_bytes=60 * 2**20
        ),
    )(*arguments)
    results = pl.pallas_call(
        finish,
        out_shape=(
            jax.ShapeDtypeStruct((nodes, width), BF),
            jax.ShapeDtypeStruct((feats, width), F32),
            jax.ShapeDtypeStruct((feats, width), F32),
            jax.ShapeDtypeStruct((1, width), F32),
            jax.ShapeDtypeStruct((width, width), F32),
            jax.ShapeDtypeStruct((width, width), F32),
            jax.ShapeDtypeStruct((1, width), F32),
        ),
        in_specs=[pl.BlockSpec(memory_space=pltpu.HBM)] * 4,
        out_specs=[pl.BlockSpec(memory_space=pltpu.HBM)] * 7,
        scratch_shapes=[
            vmem((nodes, width), BF),
            vmem((2, feats, width), TRAVEL),
            vmem((2, feats, width // 2), TRAVEL),
            vmem((1, 2 * width), F32),
            vmem((feats, width), F32),
            vmem((feats, width), F32),
            vmem((width, width), F32),
            vmem((width, width), F32),
            pltpu.SemaphoreType.DMA((11,)),
        ],
        compiler_params=pltpu.CompilerParams(vmem_limit_bytes=60 * 2**20),
    )(*summed)
    return (
        results[0],
        results[1],
        results[2],
        results[3].reshape(width),
        results[4],
        results[5],
        results[6].reshape(width),
    )


def solution(mesh):
    in_specs = (
        P(("dp", "coop"), None),
        P(),
        P(),
        P(),
        P(),
        P(),
        P(),
        P(("dp", "coop"), None, None),
        P(("dp", "coop"), None),
        P(("dp", "coop"), None, None),
        P(("dp", "coop"), None),
        P(("dp", "coop"), None, None),
        P(("dp", "coop")),
        P(("dp", "coop")),
    )
    out_specs = (
        P(("dp", "coop"), None),
        P("dp", None),
        P("dp", None),
        P("dp"),
        P("dp", None),
        P("dp", None),
        P("dp"),
    )
    return jax.shard_map(
        per_device, mesh=mesh, in_specs=in_specs, out_specs=out_specs, check_vma=False
    )
```
